512 devices in a mesh: img: 16 (over y, core), proj: 32 (over z, x).
Axes of the slice: x: 4, y: 8, z: 8, core: 2. Of those that a mesh axis runs over, the one named last changes fastest.
Arguments:
- images: bfloat16 [2048, 4096], P('img'), may hold values from -48 to 48
- projections: bfloat16 [2560, 4096], P('proj'), may hold values from -6 to 6
- noise_weight: float32 [4096], replicated, may hold values from 0.02 to 0.08
- defocus: float32 [2048], P('img'), may hold values from 2 to 8
- orient_count: int32 [2048], P('img'), may hold values from 160 to 2560, as said below
- term_limit: int32 [2048], P('img'), may hold values from 2048 to 4096
- block_plan: int32 [64], replicated, may hold values from 0 to 63, each once
Outputs:
- reconstruction: bfloat16 [2560, 4096], P('proj', 'img')
- evidence_next: float32 [2048], P('img')
The draws below stay inside these ranges and needn't reach their ends.
Inputs may be any that keep to these rules, and one draw needn't show every extreme that they name: Orientations 0 to orient_count[i] - 1 are the significant ones of image i; some image has all 2560.
All inputs are finite; a program needn't handle non-finite values.
Results may differ from the reference program's by a relative error of at most 0.018.
Values may be sent and summed in bfloat16 or wider, within the bound.
No kernel may reach another device: no remote copies, remote signals or barrier semaphores. Data moves between devices by JAX's collectives and lax.ppermute only.
A program may use at most 64 MiB of HBM per device.

```python
import math
import jax
import jax.numpy as jnp
from jax import lax

F = 4096
NPROJ = 2560
IMG_DEV = 128
BLOCK = 32
NIMG = 2048
NBLK = 64
N_IMG = 16


def shared_draw(key):
    projections = jnp.clip(jax.random.normal(jax.random.fold_in(key, 101), (NPROJ, F), jnp.float32), -6.0, 6.0)
    defocus = jax.random.uniform(jax.random.fold_in(key, 102), (NIMG,), jnp.float32, 2.0, 8.0)
    pixels = jnp.clip(jax.random.normal(jax.random.fold_in(key, 103), (NIMG, F), jnp.float32), -6.0, 6.0)
    return (projections, defocus, pixels)


def draw_projections(key, part):
    return shared_draw(key)[0].astype(jnp.bfloat16)


def draw_defocus(key, part):
    return shared_draw(key)[1]


def draw_images(key, part):
    projections, defocus, pixels = shared_draw(key)
    row_ids = jnp.arange(NIMG, dtype=jnp.int32)
    chosen = row_ids % 16 == 5
    first_pick = jax.random.randint(jax.random.fold_in(key, 105), (NIMG,), 0, max(NPROJ // 16 - 1, 1))
    second_pick = first_pick + 1
    strength = jnp.array([2.0, 3.0, 4.0], jnp.float32)[row_ids // 16 % 3]
    frequency = (jnp.arange(F, dtype=jnp.float32) + 1.0) / F
    contrast = jnp.sin(2.0 * math.pi * defocus[:, None] * frequency[None, :] + 0.1)
    aligned = strength[:, None] * contrast * (projections[first_pick] + projections[second_pick])
    pixels = jnp.where(chosen[:, None], aligned, pixels)
    return pixels.astype(jnp.bfloat16)


def draw_orient_count(key, part):
    lowest = NPROJ // 16
    level = jax.random.randint(jax.random.fold_in(key, 201), (NIMG // IMG_DEV,), lowest, NPROJ + 1)
    level = jnp.repeat(level, IMG_DEV)
    spread = jax.random.randint(jax.random.fold_in(key, 202), (NIMG,), 0, 1 << 20)
    counts = lowest + spread % (level - lowest + 1)
    return counts.at[0].set(NPROJ).astype(jnp.int32)


def place_ends(values, stream_key, smallest, high):
    shape = values.shape
    place = [jax.random.randint(jax.random.fold_in(stream_key, axis), (), 0, shape[axis]) for axis in range(len(shape))]
    values = values.at[tuple(place)].set(smallest)
    longest = shape.index(max(shape))
    place[longest] = (place[longest] + 1) % shape[longest]
    return values.at[tuple(place)].set(high)


def setup_inputs(seed: int = 0) -> dict:
    streams_of = jax.random.split(jax.random.key(seed), 8)
    return {
        "images": draw_images(jax.random.fold_in(streams_of[7], 71), 0),
        "projections": draw_projections(jax.random.fold_in(streams_of[7], 71), 0),
        "noise_weight": jnp.clip(jnp.exp(jax.random.uniform(streams_of[2], (F,), jnp.float32, math.log(0.02), math.log(0.08))), 0.02, 0.08),
        "defocus": draw_defocus(jax.random.fold_in(streams_of[7], 71), 0),
        "orient_count": draw_orient_count(jax.random.fold_in(streams_of[7], 71), 0),
        "term_limit": place_ends(jax.random.randint(streams_of[5], (NIMG,), F // 2, F + 1), jax.random.fold_in(streams_of[5], 1), F // 2, F).astype(jnp.int32),
        "block_plan": jax.random.permutation(streams_of[6], NBLK).astype(jnp.int32),
    }


def contrast_table(defocus, width):
    frequency = (jnp.arange(width, dtype=jnp.float32) + 1.0) / width
    return jnp.sin(2.0 * math.pi * defocus[:, None] * frequency[None, :] + 0.1)


def image_terms(pixels, noise_weight, defocus, limits):
    width = pixels.shape[1]
    contrast = contrast_table(defocus, width)
    keep_mask = (jnp.arange(width, dtype=jnp.int32)[None, :] < limits[:, None]).astype(contrast.dtype)
    values = pixels.astype(contrast.dtype)
    weighted = (keep_mask * noise_weight[None, :] * contrast * values).astype(jnp.bfloat16)
    weighted_sq = (keep_mask * noise_weight[None, :] * contrast * contrast).astype(jnp.bfloat16)
    back_images = (keep_mask * contrast * values).astype(jnp.bfloat16)
    back_weights = (keep_mask * contrast * contrast).astype(jnp.bfloat16)
    return weighted, weighted_sq, back_images, back_weights


def reference(images, projections, noise_weight, defocus, orient_count, term_limit, block_plan):
    wide = projections.astype(jnp.float32)
    proj_sq = (wide * wide).astype(jnp.bfloat16)
    orient_ids = jnp.arange(NPROJ, dtype=jnp.int32)

    def one_block(totals, segment):
        pixels, focus, counts, limits = segment
        weighted, weighted_sq, back_images, back_weights = image_terms(pixels, noise_weight, focus, limits)
        scores = jnp.dot(projections, weighted.T, preferred_element_type=jnp.float32)
        scores = scores - 0.5 * jnp.dot(proj_sq, weighted_sq.T, preferred_element_type=jnp.float32)
        significant = orient_ids[:, None] < counts[None, :]
        row_peak = jnp.max(jnp.where(significant, scores, -1e30), axis=0)
        safe = jnp.where(significant, scores, row_peak[None, :])
        row_mass = jnp.sum(jnp.where(significant, jnp.exp(safe - row_peak[None, :]), 0.0), axis=0)
        log_evidence = row_peak + jnp.log(row_mass)
        posterior = jnp.where(significant, jnp.exp(safe - log_evidence[None, :]), 0.0).astype(jnp.bfloat16)
        part_images = jnp.dot(posterior, back_images, preferred_element_type=jnp.float32).astype(jnp.bfloat16)
        part_weights = jnp.dot(posterior, back_weights, preferred_element_type=jnp.float32).astype(jnp.bfloat16)
        part_images = lax.optimization_barrier(part_images).astype(totals[0].dtype)
        part_weights = lax.optimization_barrier(part_weights).astype(totals[1].dtype)
        return (totals[0] + part_images, totals[1] + part_weights), log_evidence

    segments = (images.reshape(N_IMG, IMG_DEV, F), defocus.reshape(N_IMG, IMG_DEV),
                orient_count.reshape(N_IMG, IMG_DEV), term_limit.reshape(N_IMG, IMG_DEV))
    empty_sum = jnp.zeros((NPROJ, F), jnp.float32)
    (sum_images, sum_weights), evidence = lax.scan(one_block, (empty_sum, empty_sum), segments)
    reconstruction = (sum_images / (sum_weights + 1.0)).astype(jnp.bfloat16)
    evidence = evidence.reshape(NBLK, BLOCK)
    placed = jnp.zeros_like(evidence).at[block_plan].set(evidence)
    return reconstruction, placed.reshape(NIMG)
```

```python
import functools
import math

import jax
import jax.numpy as jnp
from jax import lax
from jax.experimental import pallas as pl
from jax.experimental.pallas import tpu as pltpu
from jax.sharding import PartitionSpec as P

F = 4096
BLOCK = 32
LANES = 128
COLS = 256
PAD = 16
BF = jnp.bfloat16
F32 = jnp.float32


def small_sin_cos(x):
    y = x * x
    s = 1.0
    for k in (12, 10, 8, 6, 4, 2):
        s = 1.0 - y * s * (1.0 / (k * (k + 1)))
    c = 1.0
    for k in (14, 12, 10, 8, 6, 4, 2):
        c = 1.0 - y * c * (1.0 / (k * (k - 1)))
    return x * s, c


def down_rows(row):
    n = row.shape[1]
    return jnp.transpose(jnp.broadcast_to(row, (n, n)))


def score_kernel(pixels, proj, noise, defocus, counts, limits, scores, stats, back, terms, terms_sq, turn, edge):
    rows, images = proj.shape[0], pixels.shape[0]
    lane = lax.broadcasted_iota(jnp.int32, (images, LANES), 1).astype(F32)
    angle = down_rows(defocus[...]) * ((lane + 1.0) * (2.0 * math.pi / F))
    base_s, base_c = small_sin_cos(angle)
    turn[0] = base_s * math.cos(0.1) + base_c * math.sin(0.1)
    turn[1] = base_c * math.cos(0.1) - base_s * math.sin(0.1)
    turn[2] = jnp.broadcast_to(base_s[:, LANES - 1 :], (images, LANES))
    turn[3] = jnp.broadcast_to(base_c[:, LANES - 1 :], (images, LANES))
    edge[...] = down_rows(limits[...].astype(F32)) - lane

    total = jnp.zeros((rows, images), F32)
    total_sq = jnp.zeros((rows, images), F32)
    contract = (((1,), (1,)), ((), ()))
    steps = COLS // LANES
    for g in range(F // COLS):
        for r in range(0, images, 16):
            some = slice(r, r + 16)
            s, c = turn[0, some], turn[1, some]
            step_s, step_c = turn[2, some], turn[3, some]
            last = edge[some]
            for h in range(steps):
                t = g * steps + h
                at = slice(t * LANES, (t + 1) * LANES)
                inner = slice(h * LANES, (h + 1) * LANES)
                kept = jnp.where(last > float(t * LANES), s, 0.0)
                image = kept * pixels[some, at].astype(F32)
                square = kept * s
                weight = noise[:, at]
                back[g, 0, some, inner] = image.astype(BF)
                back[g, 1, some, inner] = square.astype(BF)
                terms[some, at] = (weight * image).astype(BF)
                terms_sq[some, at] = (weight * square).astype(BF)
                s, c = s * step_c + c * step_s, c * step_c - s * step_s
            turn[0, some], turn[1, some] = s, c
        at = slice(g * COLS, (g + 1) * COLS)
        some_proj = proj[:, at]
        wide = some_proj.astype(F32)
        total += lax.dot_general(some_proj, terms[:, at], contract, preferred_element_type=F32)
        total_sq += lax.dot_general((wide * wide).astype(BF), terms_sq[:, at], contract, preferred_element_type=F32)
    found = total - 0.5 * total_sq
    orient = lax.axis_index("proj") * rows + lax.broadcasted_iota(jnp.int32, (rows, images), 0)
    significant = orient < counts[...]
    found = jnp.where(significant, found, -1e30)
    peak = jnp.max(found, axis=0, keepdims=True)
    mass = jnp.sum(jnp.where(significant, jnp.exp(found - peak), 0.0), axis=0, keepdims=True)
    scores[...] = found
    both = jnp.concatenate([peak, mass], axis=0)
    stats[...] = jnp.broadcast_to(both[None], stats.shape)


def thirds(x):
    first = x.astype(BF)
    rest = x - first.astype(F32)
    second = rest.astype(BF)
    return first, second, (rest - second.astype(F32)).astype(BF)


def back_kernel(scores, stats, back, counts, own, other):
    rows, images = scores.shape
    peaks, masses = stats[:, 0, :], stats[:, 1, :]
    peak = jnp.max(peaks, axis=0, keepdims=True)
    mass = jnp.sum(masses * jnp.exp(peaks - peak), axis=0, keepdims=True)
    evidence = peak + jnp.log(mass)
    orient = lax.axis_index("proj") * rows + lax.broadcasted_iota(jnp.int32, (rows, images), 0)
    significant = orient < counts[...]
    posterior = jnp.where(significant, jnp.exp(scores[...] - evidence), 0.0).astype(BF)
    core = lax.rem(lax.axis_index("img"), 2)
    here = lax.broadcasted_iota(jnp.int32, (PAD, COLS), 1) // LANES == core
    line = lax.broadcasted_iota(jnp.int32, (PAD, COLS), 0)
    wide = jnp.concatenate([evidence, evidence], axis=1)
    note = jnp.zeros((PAD, COLS), F32)
    for k, part in enumerate(thirds(wide)):
        note = jnp.where(line == k, part.astype(F32), note)
    note = jnp.where(here, note, 0.0).astype(BF)
    for out, side in ((own, core), (other, 1 - core)):
        for y in range(own.shape[0]):
            for k in range(2):
                part = jnp.dot(posterior, back[2 * y + side, k], preferred_element_type=F32)
                out[y, k * rows : (k + 1) * rows, :] = part.astype(BF)
            out[y, 2 * rows :, :] = note


def last_kernel(parts, plan, reconstruction, evidence):
    rows = reconstruction.shape[0]
    chips = parts.shape[0]
    images = parts[0, :rows, :].astype(F32)
    weights = parts[0, rows : 2 * rows, :].astype(F32)
    for y in range(1, chips):
        images += parts[y, :rows, :].astype(F32)
        weights += parts[y, rows : 2 * rows, :].astype(F32)
    reconstruction[...] = (images / (weights + 1.0)).astype(BF)
    lines = []
    for y in range(chips):
        note = parts[y, 2 * rows :, :].astype(F32)
        full = (note[0:1] + note[1:2]) + note[2:3]
        lines += [full[:, :LANES], full[:, LANES:]]
    known = jnp.concatenate(lines, axis=0)
    line = lax.broadcasted_iota(jnp.int32, known.shape, 0)
    group = lax.broadcasted_iota(jnp.int32, known.shape, 1) // BLOCK
    per_line = LANES // BLOCK
    number = line * per_line + group
    target = jnp.zeros(known.shape, jnp.int32)
    for b in range(2 * chips * per_line):
        target = jnp.where(number == b, plan[b], target)
    slot = lax.axis_index("img") * per_line + group
    placed = jnp.zeros((1, LANES), F32)
    for k in range(per_line):
        moved = known if k == 0 else pltpu.roll(known, k * BLOCK, 1)
        goal = target if k == 0 else pltpu.roll(target, k * BLOCK, 1)
        placed += jnp.sum(jnp.where(goal == slot, moved, 0.0), axis=0, keepdims=True)
    evidence[...] = placed


def vmem(n):
    return [pl.BlockSpec(memory_space=pltpu.VMEM)] * n


def shards(images, projections, noise_weight, defocus, orient_count, term_limit, block_plan):
    rows, count = projections.shape[0], images.shape[0]
    devices, peers = lax.axis_size("img"), lax.axis_size("proj")
    chips = devices // 2
    limit = pltpu.CompilerParams(vmem_limit_bytes=48 * 2**20)
    counts = orient_count.reshape(1, count)
    scores, stats, back = pl.pallas_call(
        score_kernel,
        name="score",
        out_shape=(
            jax.ShapeDtypeStruct((rows, count), F32),
            jax.ShapeDtypeStruct((peers, 2, count), F32),
            jax.ShapeDtypeStruct((devices, 2, count, COLS), BF),
        ),
        in_specs=vmem(6),
        out_specs=tuple(vmem(3)),
        scratch_shapes=[
            pltpu.VMEM((count, F), BF),
            pltpu.VMEM((count, F), BF),
            pltpu.VMEM((4, count, LANES), F32),
            pltpu.VMEM((count, LANES), F32),
        ],
        compiler_params=limit,
    )(
        images,
        projections,
        noise_weight.reshape(1, F),
        defocus.reshape(1, count),
        counts,
        term_limit.reshape(1, count),
    )
    stats = lax.all_to_all(stats, "proj", 0, 0, tiled=True)
    shape = jax.ShapeDtypeStruct((chips, 2 * rows + PAD, COLS), BF)
    own, other = pl.pallas_call(
        back_kernel,
        name="back",
        out_shape=(shape, shape),
        in_specs=vmem(4),
        out_specs=tuple(vmem(2)),
        compiler_params=limit,
    )(scores, stats, back, counts)
    other = lax.ppermute(other, "img", [(i, i ^ 1) for i in range(devices)])
    both = (own.astype(F32) + other.astype(F32)).astype(BF)
    same_core = [[2 * y + c for y in range(chips)] for c in range(2)]
    parts = lax.all_to_all(both, "img", 0, 0, tiled=True, axis_index_groups=same_core)
    reconstruction, evidence = pl.pallas_call(
        last_kernel,
        name="last",
        out_shape=(
            jax.ShapeDtypeStruct((rows, COLS), BF),
            jax.ShapeDtypeStruct((1, count), F32),
        ),
        in_specs=[*vmem(1), pl.BlockSpec(memory_space=pltpu.SMEM)],
        out_specs=tuple(vmem(2)),
        compiler_params=limit,
    )(parts, block_plan)
    return reconstruction, evidence.reshape(count)


def solution(mesh):
    placed = (P("img", None), P("proj", None), P(), P("img"), P("img"), P("img"), P())
    return jax.shard_map(
        shards, mesh=mesh, in_specs=placed, out_specs=(P("proj", "img"), P("img")), check_vma=False
    )
```

```python
import functools
import math

import jax
import jax.numpy as jnp
from jax import lax
from jax.experimental import pallas as pl
from jax.experimental.pallas import tpu as pltpu
from jax.sharding import PartitionSpec as P

F = 4096
BLOCK = 32
LANES = 128
COLS = 256
PAD = 8
PARTS = 8
BF = jnp.bfloat16
F32 = jnp.float32


def small_sin_cos(x):
    y = x * x
    s = 1.0
    for k in (12, 10, 8, 6, 4, 2):
        s = 1.0 - y * s * (1.0 / (k * (k + 1)))
    c = 1.0
    for k in (14, 12, 10, 8, 6, 4, 2):
        c = 1.0 - y * c * (1.0 / (k * (k - 1)))
    return x * s, c


def down_rows(row):
    n = row.shape[1]
    return jnp.transpose(jnp.broadcast_to(row, (n, n)))


def set_turn(defocus, limits, turn, edge):
    images = turn.shape[1]
    lane = lax.broadcasted_iota(jnp.int32, (images, LANES), 1).astype(F32)
    angle = down_rows(defocus) * ((lane + 1.0) * (2.0 * math.pi / F))
    base_s, base_c = small_sin_cos(angle)
    first_s = base_s * math.cos(0.1) + base_c * math.sin(0.1)
    first_c = base_c * math.cos(0.1) - base_s * math.sin(0.1)
    step_s = jnp.broadcast_to(base_s[:, LANES - 1 :], (images, LANES))
    step_c = jnp.broadcast_to(base_c[:, LANES - 1 :], (images, LANES))
    turn[0] = first_s
    turn[1] = first_s * step_c - first_c * step_s
    turn[2] = step_c + step_c
    edge[...] = down_rows(limits.astype(F32)) - lane


def walk(g, pixels, turn, edge, use):
    for r in range(0, pixels.shape[0], 16):
        some = slice(r, r + 16)
        s, before = turn[0, some], turn[1, some]
        twice = turn[2, some]
        last = edge[some]
        for h in range(COLS // LANES):
            first = g * COLS + h * LANES
            at = slice(first, first + LANES)
            kept = jnp.where(last > float(first), s, 0.0)
            use(some, at, slice(h * LANES, (h + 1) * LANES), kept * pixels[some, at].astype(F32), kept * s)
            s, before = twice * s - before, s
        turn[0, some], turn[1, some] = s, before


def score_kernel(
    far_pixels, far_proj, far_noise, far_defocus, far_counts, far_limits, scores, stats,
    pixels, proj, noise, defocus, counts, limits, terms, terms_sq, turn, edge, arrived, small_arrived,
):
    rows, images = proj.shape[0], pixels.shape[0]
    small = [
        pltpu.make_async_copy(far, near, small_arrived.at[k])
        for k, (far, near) in enumerate(
            ((far_defocus, defocus), (far_limits, limits), (far_noise, noise), (far_counts, counts))
        )
    ]
    for copy in small:
        copy.start()
    copies = []
    for n in range(PARTS):
        at = pl.ds(n * (F // PARTS), F // PARTS)
        copies.append(
            [
                pltpu.make_async_copy(far.at[:, at], near.at[:, at], arrived.at[k, n])
                for k, (far, near) in enumerate(((far_pixels, pixels), (far_proj, proj)))
            ]
        )
        for copy in copies[-1]:
            copy.start()
    for copy in small:
        copy.wait()
    set_turn(defocus[...], limits[...], turn, edge)

    def use(some, at, inner, image, square):
        weight = noise[:, at]
        terms[some, at] = (weight * image).astype(BF)
        terms_sq[some, at] = ((-0.5 * weight) * square).astype(BF)

    total = jnp.zeros((rows, images), F32)
    contract = (((1,), (1,)), ((), ()))
    groups = F // COLS
    for g in range(groups):
        if g % (groups // PARTS) == 0:
            for copy in copies[g // (groups // PARTS)]:
                copy.wait()
        walk(g, pixels, turn, edge, use)
        at = slice(g * COLS, (g + 1) * COLS)
        some_proj = proj[:, at]
        wide = some_proj.astype(F32)
        total += lax.dot_general(some_proj, terms[:, at], contract, preferred_element_type=F32)
        total += lax.dot_general((wide * wide).astype(BF), terms_sq[:, at], contract, preferred_element_type=F32)
    orient = lax.axis_index("proj") * rows + lax.broadcasted_iota(jnp.int32, (rows, images), 0)
    significant = orient < counts[...]
    found = jnp.where(significant, total, -1e30)
    peak = jnp.max(found, axis=0, keepdims=True)
    mass = jnp.sum(jnp.where(significant, jnp.exp(found - peak), 0.0), axis=0, keepdims=True)
    scores[...] = found
    both = jnp.concatenate([peak, mass], axis=0)
    stats[...] = jnp.broadcast_to(both[None], stats.shape)


def terms_kernel(far_pixels, defocus, limits, plan, back, chosen, pixels, turn, edge, arrived):
    copy = pltpu.make_async_copy(far_pixels, pixels, arrived)
    copy.start()
    set_turn(defocus[...], limits[...], turn, edge)
    copy.wait()
    for g in range(F // COLS):

        def use(some, at, inner, image, square):
            back[g, 0, some, inner] = image.astype(BF)
            back[g, 1, some, inner] = square.astype(BF)

        walk(g, pixels, turn, edge, use)
    per_line = LANES // BLOCK
    shape = chosen.shape[1:]
    blocks = plan.shape[1]
    line = lax.broadcasted_iota(jnp.int32, (shape[0], blocks), 0)
    number = lax.broadcasted_iota(jnp.int32, (shape[0], blocks), 1)
    group = lax.broadcasted_iota(jnp.int32, shape, 1) // BLOCK
    goal = jnp.broadcast_to(plan[...], (shape[0], blocks)).astype(F32)
    target = jnp.zeros(shape, F32)
    for k in range(per_line):
        mine = jnp.sum(jnp.where(number == line * per_line + k, goal, 0.0), axis=1, keepdims=True)
        target = jnp.where(group == k, mine, target)
    slot = (lax.axis_index("img") * per_line + group).astype(F32)
    for k in range(per_line):
        moved = target if k == 0 else pltpu.roll(target, k * BLOCK, 1)
        chosen[k] = jnp.where(moved == slot, 1.0, 0.0)


def thirds(x):
    first = x.astype(BF)
    rest = x - first.astype(F32)
    second = rest.astype(BF)
    return first, second, (rest - second.astype(F32)).astype(BF)


def back_kernel(scores, stats, back, counts, own, other):
    rows, images = scores.shape
    peaks, masses = stats[:, 0, :], stats[:, 1, :]
    peak = jnp.max(peaks, axis=0, keepdims=True)
    mass = jnp.sum(masses * jnp.exp(peaks - peak), axis=0, keepdims=True)
    evidence = peak + jnp.log(mass)
    orient = lax.axis_index("proj") * rows + lax.broadcasted_iota(jnp.int32, (rows, images), 0)
    significant = orient < counts[...]
    posterior = jnp.where(significant, jnp.exp(scores[...] - evidence), 0.0).astype(BF)
    core = lax.rem(lax.axis_index("img"), 2)
    here = lax.broadcasted_iota(jnp.int32, (PAD, COLS), 1) // LANES == core
    line = lax.broadcasted_iota(jnp.int32, (PAD, COLS), 0)
    wide = jnp.concatenate([evidence, evidence], axis=1)
    note = jnp.zeros((PAD, COLS), F32)
    for k, part in enumerate(thirds(wide)):
        note = jnp.where(line == k, part.astype(F32), note)
    note = jnp.where(here, note, 0.0).astype(BF)
    for out, side in ((own, core), (other, 1 - core)):
        for y in range(own.shape[0]):
            for k in range(2):
                part = jnp.dot(posterior, back[2 * y + side, k], preferred_element_type=F32)
                out[y, k * rows : (k + 1) * rows, :] = part.astype(BF)
            out[y, 2 * rows :, :] = note


def last_kernel(parts, chosen, far_reconstruction, far_evidence, reconstruction, evidence, sent):
    rows = reconstruction.shape[0]
    chips = parts.shape[0]
    images = parts[0, :rows, :].astype(F32)
    weights = parts[0, rows : 2 * rows, :].astype(F32)
    for y in range(1, chips):
        images += parts[y, :rows, :].astype(F32)
        weights += parts[y, rows : 2 * rows, :].astype(F32)
    reconstruction[...] = (images / (weights + 1.0)).astype(BF)
    first = pltpu.make_async_copy(reconstruction, far_reconstruction, sent.at[0])
    first.start()
    lines = []
    for y in range(chips):
        note = parts[y, 2 * rows :, :].astype(F32)
        full = (note[0:1] + note[1:2]) + note[2:3]
        lines += [full[:, :LANES], full[:, LANES:]]
    known = jnp.concatenate(lines, axis=0)
    placed = jnp.zeros((1, LANES), F32)
    for k in range(LANES // BLOCK):
        moved = known if k == 0 else pltpu.roll(known, k * BLOCK, 1)
        placed += jnp.sum(jnp.where(chosen[k] > 0.0, moved, 0.0), axis=0, keepdims=True)
    evidence[...] = placed
    second = pltpu.make_async_copy(evidence, far_evidence, sent.at[1])
    second.start()
    first.wait()
    second.wait()


def kept_far(array):
    return pltpu.with_memory_space_constraint(array, pltpu.HBM)


def vmem(n):
    return [pl.BlockSpec(memory_space=pltpu.VMEM)] * n


def shards(images, projections, noise_weight, defocus, orient_count, term_limit, block_plan):
    rows, count = projections.shape[0], images.shape[0]
    devices, peers = lax.axis_size("img"), lax.axis_size("proj")
    chips = devices // 2
    limit = pltpu.CompilerParams(vmem_limit_bytes=48 * 2**20)
    counts = orient_count.reshape(1, count)
    focus, limits = defocus.reshape(1, count), term_limit.reshape(1, count)
    tables = [pltpu.VMEM((3, count, LANES), F32), pltpu.VMEM((count, LANES), F32)]
    scores, stats = pl.pallas_call(
        score_kernel,
        name="score",
        out_shape=(
            jax.ShapeDtypeStruct((rows, count), F32),
            jax.ShapeDtypeStruct((peers, 2, count), F32),
        ),
        in_specs=[pl.BlockSpec(memory_space=pltpu.HBM)] * 6,
        out_specs=tuple(vmem(2)),
        scratch_shapes=[
            pltpu.VMEM((count, F), BF),
            pltpu.VMEM((rows, F), BF),
            pltpu.VMEM((1, F), F32),
            pltpu.VMEM((1, count), F32),
            pltpu.VMEM((1, count), jnp.int32),
            pltpu.VMEM((1, count), jnp.int32),
            pltpu.VMEM((count, F), BF),
            pltpu.VMEM((count, F), BF),
            *tables,
            pltpu.SemaphoreType.DMA((2, PARTS)),
            pltpu.SemaphoreType.DMA((4,)),
        ],
        compiler_params=limit,
    )(*map(kept_far, (images, projections, noise_weight.reshape(1, F), focus, counts, limits)))
    back, chosen = pl.pallas_call(
        terms_kernel,
        name="terms",
        out_shape=(
            jax.ShapeDtypeStruct((devices, 2, count, COLS), BF),
            jax.ShapeDtypeStruct((LANES // BLOCK, devices, LANES), F32),
        ),
        in_specs=[pl.BlockSpec(memory_space=pltpu.HBM), *vmem(3)],
        out_specs=tuple(vmem(2)),
        scratch_shapes=[pltpu.VMEM((count, F), BF), *tables, pltpu.SemaphoreType.DMA],
        compiler_params=limit,
        cost_estimate=pl.CostEstimate(flops=20 * count * F, bytes_accessed=6 * count * F, transcendentals=0),
    )(kept_far(images), focus, limits, block_plan.reshape(1, -1))
    stats = lax.all_to_all(stats, "proj", 0, 0, tiled=True)
    shape = jax.ShapeDtypeStruct((chips, 2 * rows + PAD, COLS), BF)
    own, other = pl.pallas_call(
        back_kernel,
        name="back",
        out_shape=(shape, shape),
        in_specs=vmem(4),
        out_specs=tuple(vmem(2)),
        compiler_params=limit,
    )(scores, stats, back, counts)
    other = lax.ppermute(other, "img", [(i, i ^ 1) for i in range(devices)])
    both = (own.astype(F32) + other.astype(F32)).astype(BF)
    same_core = [[2 * y + c for y in range(chips)] for c in range(2)]
    parts = lax.all_to_all(both, "img", 0, 0, tiled=True, axis_index_groups=same_core)
    reconstruction, evidence = pl.pallas_call(
        last_kernel,
        name="last",
        out_shape=(
            jax.ShapeDtypeStruct((rows, COLS), BF),
            jax.ShapeDtypeStruct((1, count), F32),
        ),
        in_specs=vmem(2),
        out_specs=tuple([pl.BlockSpec(memory_space=pltpu.HBM)] * 2),
        scratch_shapes=[
            pltpu.VMEM((rows, COLS), BF),
            pltpu.VMEM((1, count), F32),
            pltpu.SemaphoreType.DMA((2,)),
        ],
        compiler_params=limit,
    )(parts, chosen)
    return reconstruction, evidence.reshape(count)


def solution(mesh):
    placed = (P("img", None), P("proj", None), P(), P("img"), P("img"), P("img"), P())
    return jax.shard_map(
        shards, mesh=mesh, in_specs=placed, out_specs=(P("proj", "img"), P("img")), check_vma=False
    )
```

```python
import functools
import math

import jax
import jax.numpy as jnp
from jax import lax
from jax.experimental import pallas as pl
from jax.experimental.pallas import tpu as pltpu
from jax.sharding import PartitionSpec as P

F = 4096
BLOCK = 32
LANES = 128
COLS = 256
PAD = 8
NONE = -1e30
BF = jnp.bfloat16
F32 = jnp.float32


def small_sin_cos(x):
    y = x * x
    s = 1.0
    for k in (12, 10, 8, 6, 4, 2):
        s = 1.0 - y * s * (1.0 / (k * (k + 1)))
    c = 1.0
    for k in (14, 12, 10, 8, 6, 4, 2):
        c = 1.0 - y * c * (1.0 / (k * (k - 1)))
    return x * s, c


def down_rows(row):
    n = row.shape[1]
    return jnp.transpose(jnp.broadcast_to(row, (n, n)))


def set_turn(defocus, limits, turn, edge):
    images = turn.shape[1]
    lane = lax.broadcasted_iota(jnp.int32, (images, LANES), 1).astype(F32)
    angle = down_rows(defocus) * ((lane + 1.0) * (2.0 * math.pi / F))
    base_s, base_c = small_sin_cos(angle)
    first_s = base_s * math.cos(0.1) + base_c * math.sin(0.1)
    first_c = base_c * math.cos(0.1) - base_s * math.sin(0.1)
    step_s = jnp.broadcast_to(base_s[:, LANES - 1 :], (images, LANES))
    step_c = jnp.broadcast_to(base_c[:, LANES - 1 :], (images, LANES))
    turn[0] = first_s
    turn[1] = first_s * step_c - first_c * step_s
    turn[2] = step_c + step_c
    edge[...] = down_rows(limits.astype(F32)) - lane


def walk(g, pixels, turn, edge, use):
    for r in range(0, pixels.shape[0], 16):
        some = slice(r, r + 16)
        s, before = turn[0, some], turn[1, some]
        twice = turn[2, some]
        last = edge[some]
        for h in range(COLS // LANES):
            first = g * COLS + h * LANES
            at = slice(first, first + LANES)
            kept = jnp.where(last > float(first), s, 0.0)
            use(some, at, slice(h * LANES, (h + 1) * LANES), kept * pixels[some, at].astype(F32), kept * s)
            s, before = twice * s - before, s
        turn[0, some], turn[1, some] = s, before


def score_kernel(
    far_defocus, far_limits, far_pixels, far_proj, far_noise, far_counts, packed, stats,
    defocus, limits, pixels, proj, noise, counts, terms, terms_sq, turn, edge, arrived,
):
    rows, images = proj.shape[0], pixels.shape[0]
    copies = [
        pltpu.make_async_copy(far, near, arrived.at[k])
        for k, (far, near) in enumerate(
            (
                (far_defocus, defocus),
                (far_limits, limits),
                (far_pixels, pixels),
                (far_proj, proj),
                (far_noise, noise),
                (far_counts, counts),
            )
        )
    ]
    for copy in copies:
        copy.start()
    for copy in copies[:2]:
        copy.wait()
    set_turn(defocus[...], limits[...], turn, edge)
    for copy in copies[2:]:
        copy.wait()

    def use(some, at, inner, image, square):
        weight = noise[:, at]
        terms[some, at] = (weight * image).astype(BF)
        terms_sq[some, at] = ((-0.5 * weight) * square).astype(BF)

    total = jnp.zeros((rows, images), F32)
    contract = (((1,), (1,)), ((), ()))
    for g in range(F // COLS):
        walk(g, pixels, turn, edge, use)
        at = slice(g * COLS, (g + 1) * COLS)
        some_proj = proj[:, at]
        wide = some_proj.astype(F32)
        total += lax.dot_general(some_proj, terms[:, at], contract, preferred_element_type=F32)
        total += lax.dot_general((wide * wide).astype(BF), terms_sq[:, at], contract, preferred_element_type=F32)
    orient = lax.axis_index("proj") * rows + lax.broadcasted_iota(jnp.int32, (rows, images), 0)
    significant = orient < counts[...]
    found = jnp.where(significant, total, NONE)
    peak = jnp.max(found, axis=0, keepdims=True)
    mass = jnp.sum(jnp.where(significant, jnp.exp(found - peak), 0.0), axis=0, keepdims=True)
    both = jnp.concatenate([peak, mass], axis=0)
    stats[...] = jnp.broadcast_to(both[None], stats.shape)
    packed[:rows, :] = found
    line = lax.broadcasted_iota(jnp.int32, (8, images), 0)
    packed[rows:, :] = jnp.where(line == 0, defocus[...], jnp.where(line == 1, limits[...].astype(F32), 0.0))


def terms_kernel(pixels, far_pixels, packed, other_packed, plan, back, chosen, other_pixels, turn, edge, arrived):
    copy = pltpu.make_async_copy(far_pixels, other_pixels, arrived)
    copy.start()
    core = lax.rem(lax.axis_index("img"), 2)
    images = pixels.shape[0]
    rows = packed.shape[0] - 8
    for part, (source, scalars) in enumerate(((pixels, packed), (other_pixels, other_packed))):
        set_turn(scalars[rows : rows + 1, :], scalars[rows + 1 : rows + 2, :], turn, edge)
        if part == 1:
            copy.wait()
        for r in range(0, images, 16):
            some = slice(r, r + 16)
            out = slice(part * images + r, part * images + r + 16)
            s, before = turn[0, some], turn[1, some]
            twice = turn[2, some]
            one = twice * s - before
            two = twice * one - s
            s, before = jnp.where(core == 0, s, two), jnp.where(core == 0, before, one)
            last = edge[some] - (core * COLS).astype(F32)
            for y in range(back.shape[0]):
                for h in range(COLS // LANES):
                    first = 2 * y * COLS + h * LANES
                    at = pl.ds(pl.multiple_of(first + core * COLS, LANES), LANES)
                    inner = slice(h * LANES, (h + 1) * LANES)
                    kept = jnp.where(last > float(first), s, 0.0)
                    back[y, 0, out, inner] = (kept * source[some, at].astype(F32)).astype(BF)
                    back[y, 1, out, inner] = (kept * s).astype(BF)
                    s, before = twice * s - before, s
                for h in range(COLS // LANES):
                    s, before = twice * s - before, s
    per_line = LANES // BLOCK
    shape = chosen.shape[1:]
    blocks = plan.shape[1]
    line = lax.broadcasted_iota(jnp.int32, (shape[0], blocks), 0)
    number = lax.broadcasted_iota(jnp.int32, (shape[0], blocks), 1)
    group = lax.broadcasted_iota(jnp.int32, shape, 1) // BLOCK
    goal = jnp.broadcast_to(plan[...], (shape[0], blocks)).astype(F32)
    target = jnp.zeros(shape, F32)
    for k in range(per_line):
        mine = jnp.sum(jnp.where(number == line * per_line + k, goal, 0.0), axis=1, keepdims=True)
        target = jnp.where(group == k, mine, target)
    slot = (lax.axis_index("img") * per_line + group).astype(F32)
    for k in range(per_line):
        moved = target if k == 0 else pltpu.roll(target, k * BLOCK, 1)
        chosen[k] = jnp.where(moved == slot, 1.0, 0.0)


def thirds(x):
    first = x.astype(BF)
    rest = x - first.astype(F32)
    second = rest.astype(BF)
    return first, second, (rest - second.astype(F32)).astype(BF)


def evidence_of(stats):
    peaks, masses = stats[:, 0, :], stats[:, 1, :]
    peak = jnp.max(peaks, axis=0, keepdims=True)
    mass = jnp.sum(masses * jnp.exp(peaks - peak), axis=0, keepdims=True)
    return peak + jnp.log(mass)


def back_kernel(packed, other_packed, stats, back, out):
    rows = packed.shape[0] - 8
    peers = stats.shape[0] // 2
    core = lax.rem(lax.axis_index("img"), 2)
    known = [evidence_of(stats[c * peers : (c + 1) * peers]) for c in range(2)]
    mine, other = jnp.where(core == 0, known[0], known[1]), jnp.where(core == 0, known[1], known[0])
    posterior = jnp.concatenate(
        [
            jnp.where(some[:rows, :] > 0.5 * NONE, jnp.exp(some[:rows, :] - evidence), 0.0).astype(BF)
            for some, evidence in ((packed, mine), (other_packed, other))
        ],
        axis=1,
    )
    line = lax.broadcasted_iota(jnp.int32, (PAD, COLS), 0)
    note = jnp.zeros((PAD, COLS), F32)
    for k, part in enumerate(thirds(jnp.concatenate(known, axis=1))):
        note = jnp.where(line == k, part.astype(F32), note)
    note = note.astype(BF)
    for y in range(out.shape[0]):
        for k in range(2):
            part = jnp.dot(posterior, back[y, k], preferred_element_type=F32)
            out[y, k * rows : (k + 1) * rows, :] = part.astype(BF)
        out[y, 2 * rows :, :] = note


def last_kernel(parts, chosen, far_reconstruction, far_evidence, reconstruction, evidence, sent):
    rows = reconstruction.shape[0]
    chips = parts.shape[0]
    images = parts[0, :rows, :].astype(F32)
    weights = parts[0, rows : 2 * rows, :].astype(F32)
    for y in range(1, chips):
        images += parts[y, :rows, :].astype(F32)
        weights += parts[y, rows : 2 * rows, :].astype(F32)
    reconstruction[...] = (images / (weights + 1.0)).astype(BF)
    first = pltpu.make_async_copy(reconstruction, far_reconstruction, sent.at[0])
    first.start()
    lines = []
    for y in range(chips):
        note = parts[y, 2 * rows :, :].astype(F32)
        full = (note[0:1] + note[1:2]) + note[2:3]
        lines += [full[:, :LANES], full[:, LANES:]]
    known = jnp.concatenate(lines, axis=0)
    placed = jnp.zeros((1, LANES), F32)
    for k in range(LANES // BLOCK):
        moved = known if k == 0 else pltpu.roll(known, k * BLOCK, 1)
        placed += jnp.sum(jnp.where(chosen[k] > 0.0, moved, 0.0), axis=0, keepdims=True)
    evidence[...] = placed
    second = pltpu.make_async_copy(evidence, far_evidence, sent.at[1])
    second.start()
    first.wait()
    second.wait()


def kept_far(array):
    return pltpu.with_memory_space_constraint(array, pltpu.HBM)


def vmem(n):
    return [pl.BlockSpec(memory_space=pltpu.VMEM)] * n


def shards(images, projections, noise_weight, defocus, orient_count, term_limit, block_plan):
    rows, count = projections.shape[0], images.shape[0]
    devices, peers = lax.axis_size("img"), lax.axis_size("proj")
    chips = devices // 2
    limit = pltpu.CompilerParams(vmem_limit_bytes=16 * 2**20)
    focus, counts, limits = (a.reshape(1, count) for a in (defocus, orient_count, term_limit))
    tables = [pltpu.VMEM((3, count, LANES), F32), pltpu.VMEM((count, LANES), F32)]
    partners = [(i, i ^ 1) for i in range(devices)]
    other_images = lax.optimization_barrier(lax.ppermute(images, "img", partners))
    operands = (focus, limits, images, projections, noise_weight.reshape(1, F), counts)
    packed, stats = pl.pallas_call(
        score_kernel,
        name="score",
        out_shape=(
            jax.ShapeDtypeStruct((rows + 8, count), F32),
            jax.ShapeDtypeStruct((2 * peers, 2, count), F32),
        ),
        in_specs=[pl.BlockSpec(memory_space=pltpu.HBM)] * 6,
        out_specs=tuple(vmem(2)),
        scratch_shapes=[
            *(pltpu.VMEM(a.shape, a.dtype) for a in operands),
            pltpu.VMEM((count, F), BF),
            pltpu.VMEM((count, F), BF),
            *tables,
            pltpu.SemaphoreType.DMA((6,)),
        ],
        compiler_params=limit,
    )(*map(kept_far, operands))
    chip = [[2 * y * peers + n for n in range(2 * peers)] for y in range(chips)]
    stats = lax.all_to_all(stats, ("img", "proj"), 0, 0, tiled=True, axis_index_groups=chip)
    other_packed = lax.ppermute(packed, "img", partners)
    back, chosen = pl.pallas_call(
        terms_kernel,
        name="terms",
        out_shape=(
            jax.ShapeDtypeStruct((chips, 2, 2 * count, COLS), BF),
            jax.ShapeDtypeStruct((LANES // BLOCK, devices, LANES), F32),
        ),
        in_specs=[*vmem(1), pl.BlockSpec(memory_space=pltpu.HBM), *vmem(3)],
        out_specs=tuple(vmem(2)),
        scratch_shapes=[pltpu.VMEM((count, F), BF), *tables, pltpu.SemaphoreType.DMA],
        compiler_params=limit,
        cost_estimate=pl.CostEstimate(flops=20 * count * F, bytes_accessed=6 * count * F, transcendentals=0),
    )(images, kept_far(other_images), packed, other_packed, block_plan.reshape(1, -1))
    both = pl.pallas_call(
        back_kernel,
        name="back",
        out_shape=jax.ShapeDtypeStruct((chips, 2 * rows + PAD, COLS), BF),
        in_specs=vmem(4),
        out_specs=vmem(1)[0],
        compiler_params=limit,
    )(packed, other_packed, stats, back)
    same_core = [[2 * y + c for y in range(chips)] for c in range(2)]
    parts = lax.all_to_all(both, "img", 0, 0, tiled=True, axis_index_groups=same_core)
    reconstruction, evidence = pl.pallas_call(
        last_kernel,
        name="last",
        out_shape=(
            jax.ShapeDtypeStruct((rows, COLS), BF),
            jax.ShapeDtypeStruct((1, count), F32),
        ),
        in_specs=vmem(2),
        out_specs=tuple([pl.BlockSpec(memory_space=pltpu.HBM)] * 2),
        scratch_shapes=[
            pltpu.VMEM((rows, COLS), BF),
            pltpu.VMEM((1, count), F32),
            pltpu.SemaphoreType.DMA((2,)),
        ],
        compiler_params=limit,
    )(parts, chosen)
    return reconstruction, evidence.reshape(count)


def solution(mesh):
    placed = (P("img", None), P("proj", None), P(), P("img"), P("img"), P("img"), P())
    return jax.shard_map(
        shards, mesh=mesh, in_specs=placed, out_specs=(P("proj", "img"), P("img")), check_vma=False
    )
```

```python
import functools
import math

import jax
import jax.numpy as jnp
from jax import lax
from jax.experimental import pallas as pl
from jax.experimental.pallas import tpu as pltpu
from jax.sharding import PartitionSpec as P

F = 4096
BLOCK = 32
LANES = 128
COLS = 256
PAD = 8
NONE = -1e30
BF = jnp.bfloat16
F32 = jnp.float32


def small_sin_cos(x):
    y = x * x
    s = 1.0
    for k in (12, 10, 8, 6, 4, 2):
        s = 1.0 - y * s * (1.0 / (k * (k + 1)))
    c = 1.0
    for k in (14, 12, 10, 8, 6, 4, 2):
        c = 1.0 - y * c * (1.0 / (k * (k - 1)))
    return x * s, c


def down_rows(row):
    n = row.shape[1]
    return jnp.transpose(jnp.broadcast_to(row, (n, n)))


def set_turn(defocus, limits, turn, edge):
    images = turn.shape[1]
    lane = lax.broadcasted_iota(jnp.int32, (images, LANES), 1).astype(F32)
    angle = down_rows(defocus) * ((lane + 1.0) * (2.0 * math.pi / F))
    base_s, base_c = small_sin_cos(angle)
    first_s = base_s * math.cos(0.1) + base_c * math.sin(0.1)
    first_c = base_c * math.cos(0.1) - base_s * math.sin(0.1)
    step_s = jnp.broadcast_to(base_s[:, LANES - 1 :], (images, LANES))
    step_c = jnp.broadcast_to(base_c[:, LANES - 1 :], (images, LANES))
    turn[0] = first_s
    turn[1] = first_s * step_c - first_c * step_s
    turn[2] = step_c + step_c
    edge[...] = down_rows(limits.astype(F32)) - lane


def walk(g, pixels, turn, edge, use):
    for r in range(0, pixels.shape[0], 16):
        some = slice(r, r + 16)
        s, before = turn[0, some], turn[1, some]
        twice = turn[2, some]
        last = edge[some]
        for h in range(COLS // LANES):
            first = g * COLS + h * LANES
            at = slice(first, first + LANES)
            kept = jnp.where(last > float(first), s, 0.0)
            use(some, at, slice(h * LANES, (h + 1) * LANES), kept * pixels[some, at].astype(F32), kept * s)
            s, before = twice * s - before, s
        turn[0, some], turn[1, some] = s, before


def thirds(x):
    first = x.astype(BF)
    rest = x - first.astype(F32)
    second = rest.astype(BF)
    return first, second, (rest - second.astype(F32)).astype(BF)


def score_kernel(
    far_defocus, far_limits, far_pixels, far_proj, far_noise, far_counts, kept, sent, stats,
    defocus, limits, pixels, proj, noise, counts, terms, terms_sq, turn, edge, arrived,
):
    rows, images = proj.shape[0], pixels.shape[0]
    copies = [
        pltpu.make_async_copy(far, near, arrived.at[k])
        for k, (far, near) in enumerate(
            (
                (far_defocus, defocus),
                (far_limits, limits),
                (far_pixels, pixels),
                (far_proj, proj),
                (far_noise, noise),
                (far_counts, counts),
            )
        )
    ]
    for copy in copies:
        copy.start()
    for copy in copies[:2]:
        copy.wait()
    set_turn(defocus[...], limits[...], turn, edge)
    for copy in copies[2:]:
        copy.wait()

    def use(some, at, inner, image, square):
        weight = noise[:, at]
        terms[some, at] = (weight * image).astype(BF)
        terms_sq[some, at] = ((-0.5 * weight) * square).astype(BF)

    total = jnp.zeros((rows, images), F32)
    contract = (((1,), (1,)), ((), ()))
    for g in range(F // COLS):
        walk(g, pixels, turn, edge, use)
        at = slice(g * COLS, (g + 1) * COLS)
        some_proj = proj[:, at]
        wide = some_proj.astype(F32)
        total += lax.dot_general(some_proj, terms[:, at], contract, preferred_element_type=F32)
        total += lax.dot_general((wide * wide).astype(BF), terms_sq[:, at], contract, preferred_element_type=F32)
    orient = lax.axis_index("proj") * rows + lax.broadcasted_iota(jnp.int32, (rows, images), 0)
    significant = orient < counts[...]
    found = jnp.where(significant, total, NONE)
    peak = jnp.max(found, axis=0, keepdims=True)
    mass = jnp.sum(jnp.where(significant, jnp.exp(found - peak), 0.0), axis=0, keepdims=True)
    both = jnp.concatenate([peak, mass], axis=0)
    stats[...] = jnp.broadcast_to(both[None], stats.shape)
    line = lax.broadcasted_iota(jnp.int32, (rows, images), 0)
    scalars = jnp.zeros((rows, images), F32)
    for k, part in enumerate((*thirds(defocus[...]), *thirds(limits[...].astype(F32)))):
        scalars = jnp.where(line == k, part.astype(F32), scalars)
    first, second, third = thirds(found)
    core = lax.rem(lax.axis_index("img"), 2)
    groups = F // COLS // 2
    tail = groups * images
    for out, side in ((kept, core), (sent, 1 - core)):
        for y in range(groups):
            at = pl.ds(pl.multiple_of((2 * y + side) * COLS, COLS), COLS)
            out[y * images : (y + 1) * images, :] = pixels[:, at]
        out[tail : tail + rows, :LANES] = first
        out[tail : tail + rows, LANES:] = second
        out[tail + rows :, :LANES] = third
        out[tail + rows :, LANES:] = scalars.astype(BF)


def scores_of(half, rows):
    tail = half.shape[0] - 2 * rows
    first, second = half[tail : tail + rows, :LANES], half[tail : tail + rows, LANES:]
    return (first.astype(F32) + second.astype(F32)) + half[tail + rows :, :LANES].astype(F32)


def half_terms(half, rows, back, turn, edge):
    core = lax.rem(lax.axis_index("img"), 2)
    images = back.shape[2]
    start = half.shape[0] - rows
    scalars = half[start : start + 16, LANES:].astype(F32)
    focus, limits = ((scalars[k : k + 1] + scalars[k + 1 : k + 2]) + scalars[k + 2 : k + 3] for k in (0, 3))
    set_turn(focus, limits, turn, edge)
    for r in range(0, images, 16):
        some = slice(r, r + 16)
        s, before = turn[0, some], turn[1, some]
        twice = turn[2, some]
        one = twice * s - before
        two = twice * one - s
        s, before = jnp.where(core == 0, s, two), jnp.where(core == 0, before, one)
        last = edge[some] - (core * COLS).astype(F32)
        for y in range(back.shape[0]):
            for h in range(COLS // LANES):
                inner = slice(h * LANES, (h + 1) * LANES)
                kept = jnp.where(last > float(2 * y * COLS + h * LANES), s, 0.0)
                image = half[y * images + r : y * images + r + 16, inner].astype(F32)
                back[y, 0, some, inner] = (kept * image).astype(BF)
                back[y, 1, some, inner] = (kept * s).astype(BF)
                s, before = twice * s - before, s
            for h in range(COLS // LANES):
                s, before = twice * s - before, s


def other_terms_kernel(rows, half, back, turn, edge):
    half_terms(half, rows, back, turn, edge)


def own_terms_kernel(rows, half, far_plan, back, chosen, plan, turn, edge, arrived):
    copy = pltpu.make_async_copy(far_plan, plan, arrived)
    copy.start()
    half_terms(half, rows, back, turn, edge)
    copy.wait()
    per_line = LANES // BLOCK
    shape = chosen.shape[1:]
    blocks = plan.shape[1]
    line = lax.broadcasted_iota(jnp.int32, (shape[0], blocks), 0)
    number = lax.broadcasted_iota(jnp.int32, (shape[0], blocks), 1)
    group = lax.broadcasted_iota(jnp.int32, shape, 1) // BLOCK
    goal = jnp.broadcast_to(plan[...], (shape[0], blocks)).astype(F32)
    target = jnp.zeros(shape, F32)
    for k in range(per_line):
        mine = jnp.sum(jnp.where(number == line * per_line + k, goal, 0.0), axis=1, keepdims=True)
        target = jnp.where(group == k, mine, target)
    slot = (lax.axis_index("img") * per_line + group).astype(F32)
    for k in range(per_line):
        moved = target if k == 0 else pltpu.roll(target, k * BLOCK, 1)
        chosen[k] = jnp.where(moved == slot, 1.0, 0.0)


def evidence_of(stats):
    peaks, masses = stats[:, 0, :], stats[:, 1, :]
    peak = jnp.max(peaks, axis=0, keepdims=True)
    mass = jnp.sum(masses * jnp.exp(peaks - peak), axis=0, keepdims=True)
    return peak + jnp.log(mass)


def back_kernel(half, other_half, stats, back, other_back, out):
    rows = (out.shape[1] - PAD) // 2
    peers = stats.shape[0] // 2
    core = lax.rem(lax.axis_index("img"), 2)
    known = [evidence_of(stats[c * peers : (c + 1) * peers]) for c in range(2)]
    mine, other = jnp.where(core == 0, known[0], known[1]), jnp.where(core == 0, known[1], known[0])

    def posterior_of(scores, evidence):
        return jnp.where(scores > 0.5 * NONE, jnp.exp(scores - evidence), 0.0).astype(BF)

    posterior = posterior_of(scores_of(half, rows), mine)
    other_posterior = posterior_of(scores_of(other_half, rows), other)
    line = lax.broadcasted_iota(jnp.int32, (PAD, COLS), 0)
    note = jnp.zeros((PAD, COLS), F32)
    for k, part in enumerate(thirds(jnp.concatenate(known, axis=1))):
        note = jnp.where(line == k, part.astype(F32), note)
    note = note.astype(BF)
    for y in range(out.shape[0]):
        for k in range(2):
            part = jnp.dot(posterior, back[y, k], preferred_element_type=F32)
            part += jnp.dot(other_posterior, other_back[y, k], preferred_element_type=F32)
            out[y, k * rows : (k + 1) * rows, :] = part.astype(BF)
        out[y, 2 * rows :, :] = note


def last_kernel(parts, chosen, far_reconstruction, far_evidence, reconstruction, evidence, sent):
    rows = reconstruction.shape[0]
    chips = parts.shape[0]
    images = parts[0, :rows, :].astype(F32)
    weights = parts[0, rows : 2 * rows, :].astype(F32)
    for y in range(1, chips):
        images += parts[y, :rows, :].astype(F32)
        weights += parts[y, rows : 2 * rows, :].astype(F32)
    reconstruction[...] = (images / (weights + 1.0)).astype(BF)
    first = pltpu.make_async_copy(reconstruction, far_reconstruction, sent.at[0])
    first.start()
    lines = []
    for y in range(chips):
        note = parts[y, 2 * rows :, :].astype(F32)
        full = (note[0:1] + note[1:2]) + note[2:3]
        lines += [full[:, :LANES], full[:, LANES:]]
    known = jnp.concatenate(lines, axis=0)
    placed = jnp.zeros((1, LANES), F32)
    for k in range(LANES // BLOCK):
        moved = known if k == 0 else pltpu.roll(known, k * BLOCK, 1)
        placed += jnp.sum(jnp.where(chosen[k] > 0.0, moved, 0.0), axis=0, keepdims=True)
    evidence[...] = placed
    second = pltpu.make_async_copy(evidence, far_evidence, sent.at[1])
    second.start()
    first.wait()
    second.wait()


def kept_far(array):
    return pltpu.with_memory_space_constraint(array, pltpu.HBM)


def vmem(n):
    return [pl.BlockSpec(memory_space=pltpu.VMEM)] * n


def shards(images, projections, noise_weight, defocus, orient_count, term_limit, block_plan):
    rows, count = projections.shape[0], images.shape[0]
    devices, peers = lax.axis_size("img"), lax.axis_size("proj")
    chips = devices // 2
    limit = pltpu.CompilerParams(vmem_limit_bytes=16 * 2**20)
    focus, counts, limits = (a.reshape(1, count) for a in (defocus, orient_count, term_limit))
    tables = [pltpu.VMEM((3, count, LANES), F32), pltpu.VMEM((count, LANES), F32)]
    partners = [(i, i ^ 1) for i in range(devices)]
    operands = (focus, limits, images, projections, noise_weight.reshape(1, F), counts)
    shape = jax.ShapeDtypeStruct((chips * count + 2 * rows, COLS), BF)
    half, sent, stats = pl.pallas_call(
        score_kernel,
        name="score",
        out_shape=(
            shape,
            shape,
            jax.ShapeDtypeStruct((2 * peers, 2, count), F32),
        ),
        in_specs=[pl.BlockSpec(memory_space=pltpu.HBM)] * 6,
        out_specs=tuple(vmem(3)),
        scratch_shapes=[
            *(pltpu.VMEM(a.shape, a.dtype) for a in operands),
            pltpu.VMEM((count, F), BF),
            pltpu.VMEM((count, F), BF),
            *tables,
            pltpu.SemaphoreType.DMA((6,)),
        ],
        compiler_params=limit,
    )(*map(kept_far, operands))
    chip = [[2 * y * peers + n for n in range(2 * peers)] for y in range(chips)]
    stats = lax.all_to_all(stats, ("img", "proj"), 0, 0, tiled=True, axis_index_groups=chip)
    shape = jax.ShapeDtypeStruct((chips, 2, count, COLS), BF)
    cost = pl.CostEstimate(flops=10 * count * F, bytes_accessed=3 * count * F, transcendentals=0)
    back, chosen = pl.pallas_call(
        functools.partial(own_terms_kernel, rows),
        name="own_terms",
        out_shape=(shape, jax.ShapeDtypeStruct((LANES // BLOCK, devices, LANES), F32)),
        in_specs=[*vmem(1), pl.BlockSpec(memory_space=pltpu.HBM)],
        out_specs=tuple(vmem(2)),
        scratch_shapes=[pltpu.VMEM((1, block_plan.shape[0]), jnp.int32), *tables, pltpu.SemaphoreType.DMA],
        compiler_params=limit,
        cost_estimate=cost,
    )(half, kept_far(block_plan.reshape(1, -1)))
    other_half = lax.ppermute(sent, "img", partners)
    other_back = pl.pallas_call(
        functools.partial(other_terms_kernel, rows),
        name="other_terms",
        out_shape=shape,
        in_specs=vmem(1),
        out_specs=vmem(1)[0],
        scratch_shapes=tables,
        compiler_params=limit,
        cost_estimate=pl.CostEstimate(flops=1, bytes_accessed=1, transcendentals=0),
    )(other_half)
    both = pl.pallas_call(
        back_kernel,
        name="back",
        out_shape=jax.ShapeDtypeStruct((chips, 2 * rows + PAD, COLS), BF),
        in_specs=vmem(5),
        out_specs=vmem(1)[0],
        compiler_params=limit,
    )(half, other_half, stats, back, other_back)
    same_core = [[2 * y + c for y in range(chips)] for c in range(2)]
    parts = lax.all_to_all(both, "img", 0, 0, tiled=True, axis_index_groups=same_core)
    reconstruction, evidence = pl.pallas_call(
        last_kernel,
        name="last",
        out_shape=(
            jax.ShapeDtypeStruct((rows, COLS), BF),
            jax.ShapeDtypeStruct((1, count), F32),
        ),
        in_specs=vmem(2),
        out_specs=tuple([pl.BlockSpec(memory_space=pltpu.HBM)] * 2),
        scratch_shapes=[
            pltpu.VMEM((rows, COLS), BF),
            pltpu.VMEM((1, count), F32),
            pltpu.SemaphoreType.DMA((2,)),
        ],
        compiler_params=limit,
    )(parts, chosen)
    return reconstruction, evidence.reshape(count)


def solution(mesh):
    placed = (P("img", None), P("proj", None), P(), P("img"), P("img"), P("img"), P())
    return jax.shard_map(
        shards, mesh=mesh, in_specs=placed, out_specs=(P("proj", "img"), P("img")), check_vma=False
    )
```

```python
import functools
import math

import jax
import jax.numpy as jnp
from jax import lax
from jax.experimental import pallas as pl
from jax.experimental.pallas import tpu as pltpu
from jax.sharding import PartitionSpec as P

F = 4096
BLOCK = 32
LANES = 128
COLS = 256
PAD = 8
NONE = -1e30
BF = jnp.bfloat16
F32 = jnp.float32


def small_sin_cos(x):
    y = x * x
    s = 1.0
    for k in (12, 10, 8, 6, 4, 2):
        s = 1.0 - y * s * (1.0 / (k * (k + 1)))
    c = 1.0
    for k in (14, 12, 10, 8, 6, 4, 2):
        c = 1.0 - y * c * (1.0 / (k * (k - 1)))
    return x * s, c


def down_rows(row):
    n = row.shape[1]
    return jnp.transpose(jnp.broadcast_to(row, (n, n)))


def set_turn(defocus, limits, turn, edge):
    images = turn.shape[1]
    lane = lax.broadcasted_iota(jnp.int32, (images, LANES), 1).astype(F32)
    angle = down_rows(defocus) * ((lane + 1.0) * (2.0 * math.pi / F))
    base_s, base_c = small_sin_cos(angle)
    first_s = base_s * math.cos(0.1) + base_c * math.sin(0.1)
    first_c = base_c * math.cos(0.1) - base_s * math.sin(0.1)
    step_s = jnp.broadcast_to(base_s[:, LANES - 1 :], (images, LANES))
    step_c = jnp.broadcast_to(base_c[:, LANES - 1 :], (images, LANES))
    turn[0] = first_s
    turn[1] = first_s * step_c - first_c * step_s
    turn[2] = step_c + step_c
    edge[...] = down_rows(limits.astype(F32)) - lane


def walk(g, pixels, turn, edge, use):
    for r in range(0, pixels.shape[0], 16):
        some = slice(r, r + 16)
        s, before = turn[0, some], turn[1, some]
        twice = turn[2, some]
        last = edge[some]
        for h in range(COLS // LANES):
            first = g * COLS + h * LANES
            at = slice(first, first + LANES)
            kept = jnp.where(last > float(first), s, 0.0)
            use(some, at, slice(h * LANES, (h + 1) * LANES), kept * pixels[some, at].astype(F32), kept * s)
            s, before = twice * s - before, s
        turn[0, some], turn[1, some] = s, before


def thirds(x):
    first = x.astype(BF)
    rest = x - first.astype(F32)
    second = rest.astype(BF)
    return first, second, (rest - second.astype(F32)).astype(BF)


def score_kernel(
    far_defocus, far_limits, far_pixels, far_proj, far_noise, far_counts, kept, sent, stats,
    defocus, limits, pixels, proj, noise, counts, terms, terms_sq, turn, edge, arrived,
):
    rows, images = proj.shape[0], pixels.shape[0]
    copies = [
        pltpu.make_async_copy(far, near, arrived.at[k])
        for k, (far, near) in enumerate(
            (
                (far_defocus, defocus),
                (far_limits, limits),
                (far_pixels, pixels),
                (far_proj, proj),
                (far_noise, noise),
                (far_counts, counts),
            )
        )
    ]
    for copy in copies:
        copy.start()
    for copy in copies[:2]:
        copy.wait()
    set_turn(defocus[...], limits[...], turn, edge)
    for copy in copies[2:]:
        copy.wait()

    def use(some, at, inner, image, square):
        weight = noise[:, at]
        terms[some, at] = (weight * image).astype(BF)
        terms_sq[some, at] = ((-0.5 * weight) * square).astype(BF)

    sums = [jnp.zeros((rows, images), F32) for _ in range(4)]
    contract = (((1,), (1,)), ((), ()))
    for g in range(F // COLS):
        walk(g, pixels, turn, edge, use)
        at = slice(g * COLS, (g + 1) * COLS)
        some_proj = proj[:, at]
        wide = some_proj.astype(F32)
        sums[g % 2] += lax.dot_general(some_proj, terms[:, at], contract, preferred_element_type=F32)
        sums[2 + g % 2] += lax.dot_general((wide * wide).astype(BF), terms_sq[:, at], contract, preferred_element_type=F32)
    total = (sums[0] + sums[1]) + (sums[2] + sums[3])
    orient = lax.axis_index("proj") * rows + lax.broadcasted_iota(jnp.int32, (rows, images), 0)
    significant = orient < counts[...]
    found = jnp.where(significant, total, NONE)
    peak = jnp.max(found, axis=0, keepdims=True)
    mass = jnp.sum(jnp.where(significant, jnp.exp(found - peak), 0.0), axis=0, keepdims=True)
    both = jnp.concatenate([peak, mass], axis=0)
    stats[...] = jnp.broadcast_to(both[None], stats.shape)
    line = lax.broadcasted_iota(jnp.int32, (rows, images), 0)
    scalars = jnp.zeros((rows, images), F32)
    for k, part in enumerate((*thirds(defocus[...]), *thirds(limits[...].astype(F32)))):
        scalars = jnp.where(line == k, part.astype(F32), scalars)
    first, second, third = thirds(found)
    core = lax.rem(lax.axis_index("img"), 2)
    groups = F // COLS // 2
    tail = groups * images
    for out, side in ((kept, core), (sent, 1 - core)):
        for y in range(groups):
            at = pl.ds(pl.multiple_of((2 * y + side) * COLS, COLS), COLS)
            out[y * images : (y + 1) * images, :] = pixels[:, at]
        out[tail : tail + rows, :LANES] = first
        out[tail : tail + rows, LANES:] = second
        out[tail + rows :, :LANES] = third
        out[tail + rows :, LANES:] = scalars.astype(BF)


def scores_of(half, rows):
    tail = half.shape[0] - 2 * rows
    first, second = half[tail : tail + rows, :LANES], half[tail : tail + rows, LANES:]
    return (first.astype(F32) + second.astype(F32)) + half[tail + rows :, :LANES].astype(F32)


def half_terms(half, rows, back, turn, edge):
    core = lax.rem(lax.axis_index("img"), 2)
    images = back.shape[2]
    start = half.shape[0] - rows
    scalars = half[start : start + 16, LANES:].astype(F32)
    focus, limits = ((scalars[k : k + 1] + scalars[k + 1 : k + 2]) + scalars[k + 2 : k + 3] for k in (0, 3))
    set_turn(focus, limits, turn, edge)
    for r in range(0, images, 16):
        some = slice(r, r + 16)
        s, before = turn[0, some], turn[1, some]
        twice = turn[2, some]
        one = twice * s - before
        two = twice * one - s
        s, before = jnp.where(core == 0, s, two), jnp.where(core == 0, before, one)
        last = edge[some] - (core * COLS).astype(F32)
        for y in range(back.shape[0]):
            for h in range(COLS // LANES):
                inner = slice(h * LANES, (h + 1) * LANES)
                kept = jnp.where(last > float(2 * y * COLS + h * LANES), s, 0.0)
                image = half[y * images + r : y * images + r + 16, inner].astype(F32)
                back[y, 0, some, inner] = (kept * image).astype(BF)
                back[y, 1, some, inner] = (kept * s).astype(BF)
                s, before = twice * s - before, s
            for h in range(COLS // LANES):
                s, before = twice * s - before, s


def other_terms_kernel(rows, half, back, turn, edge):
    half_terms(half, rows, back, turn, edge)


def own_terms_kernel(rows, half, far_plan, back, chosen, plan, turn, edge, arrived):
    copy = pltpu.make_async_copy(far_plan, plan, arrived)
    copy.start()
    half_terms(half, rows, back, turn, edge)
    copy.wait()
    per_line = LANES // BLOCK
    shape = chosen.shape[1:]
    blocks = plan.shape[1]
    line = lax.broadcasted_iota(jnp.int32, (shape[0], blocks), 0)
    number = lax.broadcasted_iota(jnp.int32, (shape[0], blocks), 1)
    group = lax.broadcasted_iota(jnp.int32, shape, 1) // BLOCK
    goal = jnp.broadcast_to(plan[...], (shape[0], blocks)).astype(F32)
    target = jnp.zeros(shape, F32)
    for k in range(per_line):
        mine = jnp.sum(jnp.where(number == line * per_line + k, goal, 0.0), axis=1, keepdims=True)
        target = jnp.where(group == k, mine, target)
    slot = (lax.axis_index("img") * per_line + group).astype(F32)
    for k in range(per_line):
        moved = target if k == 0 else pltpu.roll(target, k * BLOCK, 1)
        chosen[k] = jnp.where(moved == slot, 1.0, 0.0)


def evidence_of(stats):
    peaks, masses = stats[:, 0, :], stats[:, 1, :]
    peak = jnp.max(peaks, axis=0, keepdims=True)
    mass = jnp.sum(masses * jnp.exp(peaks - peak), axis=0, keepdims=True)
    return peak + jnp.log(mass)


def back_kernel(half, other_half, stats, back, other_back, out):
    rows = (out.shape[1] - PAD) // 2
    peers = stats.shape[0] // 2
    core = lax.rem(lax.axis_index("img"), 2)
    known = [evidence_of(stats[c * peers : (c + 1) * peers]) for c in range(2)]
    mine, other = jnp.where(core == 0, known[0], known[1]), jnp.where(core == 0, known[1], known[0])

    def posterior_of(scores, evidence):
        return jnp.where(scores > 0.5 * NONE, jnp.exp(scores - evidence), 0.0).astype(BF)

    posterior = posterior_of(scores_of(half, rows), mine)
    other_posterior = posterior_of(scores_of(other_half, rows), other)
    line = lax.broadcasted_iota(jnp.int32, (PAD, COLS), 0)
    note = jnp.zeros((PAD, COLS), F32)
    for k, part in enumerate(thirds(jnp.concatenate(known, axis=1))):
        note = jnp.where(line == k, part.astype(F32), note)
    note = note.astype(BF)
    for y in range(out.shape[0]):
        for k in range(2):
            part = jnp.dot(posterior, back[y, k], preferred_element_type=F32)
            part += jnp.dot(other_posterior, other_back[y, k], preferred_element_type=F32)
            out[y, k * rows : (k + 1) * rows, :] = part.astype(BF)
        out[y, 2 * rows :, :] = note


def last_kernel(parts, chosen, far_reconstruction, far_evidence, reconstruction, evidence, sent):
    rows = reconstruction.shape[0]
    chips = parts.shape[0]
    images = parts[0, :rows, :].astype(F32)
    weights = parts[0, rows : 2 * rows, :].astype(F32)
    for y in range(1, chips):
        images += parts[y, :rows, :].astype(F32)
        weights += parts[y, rows : 2 * rows, :].astype(F32)
    reconstruction[...] = (images / (weights + 1.0)).astype(BF)
    first = pltpu.make_async_copy(reconstruction, far_reconstruction, sent.at[0])
    first.start()
    lines = []
    for y in range(chips):
        note = parts[y, 2 * rows :, :].astype(F32)
        full = (note[0:1] + note[1:2]) + note[2:3]
        lines += [full[:, :LANES], full[:, LANES:]]
    known = jnp.concatenate(lines, axis=0)
    placed = jnp.zeros((1, LANES), F32)
    for k in range(LANES // BLOCK):
        moved = known if k == 0 else pltpu.roll(known, k * BLOCK, 1)
        placed += jnp.sum(jnp.where(chosen[k] > 0.0, moved, 0.0), axis=0, keepdims=True)
    evidence[...] = placed
    second = pltpu.make_async_copy(evidence, far_evidence, sent.at[1])
    second.start()
    first.wait()
    second.wait()


def kept_far(array):
    return pltpu.with_memory_space_constraint(array, pltpu.HBM)


def vmem(n):
    return [pl.BlockSpec(memory_space=pltpu.VMEM)] * n


def shards(images, projections, noise_weight, defocus, orient_count, term_limit, block_plan):
    rows, count = projections.shape[0], images.shape[0]
    devices, peers = lax.axis_size("img"), lax.axis_size("proj")
    chips = devices // 2
    limit = pltpu.CompilerParams(vmem_limit_bytes=16 * 2**20)
    focus, counts, limits = (a.reshape(1, count) for a in (defocus, orient_count, term_limit))
    tables = [pltpu.VMEM((3, count, LANES), F32), pltpu.VMEM((count, LANES), F32)]
    partners = [(i, i ^ 1) for i in range(devices)]
    operands = (focus, limits, images, projections, noise_weight.reshape(1, F), counts)
    shape = jax.ShapeDtypeStruct((chips * count + 2 * rows, COLS), BF)
    half, sent, stats = pl.pallas_call(
        score_kernel,
        name="score",
        out_shape=(
            shape,
            shape,
            jax.ShapeDtypeStruct((2 * peers, 2, count), F32),
        ),
        in_specs=[pl.BlockSpec(memory_space=pltpu.HBM)] * 6,
        out_specs=tuple(vmem(3)),
        scratch_shapes=[
            *(pltpu.VMEM(a.shape, a.dtype) for a in operands),
            pltpu.VMEM((count, F), BF),
            pltpu.VMEM((count, F), BF),
            *tables,
            pltpu.SemaphoreType.DMA((6,)),
        ],
        compiler_params=limit,
    )(*map(kept_far, operands))
    chip = [[2 * y * peers + n for n in range(2 * peers)] for y in range(chips)]
    stats = lax.all_to_all(stats, ("img", "proj"), 0, 0, tiled=True, axis_index_groups=chip)
    shape = jax.ShapeDtypeStruct((chips, 2, count, COLS), BF)
    cost = pl.CostEstimate(flops=10**10, bytes_accessed=3 * count * F, transcendentals=0)
    back, chosen = pl.pallas_call(
        functools.partial(own_terms_kernel, rows),
        name="own_terms",
        out_shape=(shape, jax.ShapeDtypeStruct((LANES // BLOCK, devices, LANES), F32)),
        in_specs=[*vmem(1), pl.BlockSpec(memory_space=pltpu.HBM)],
        out_specs=tuple(vmem(2)),
        scratch_shapes=[pltpu.VMEM((1, block_plan.shape[0]), jnp.int32), *tables, pltpu.SemaphoreType.DMA],
        compiler_params=limit,
        cost_estimate=cost,
    )(half, kept_far(block_plan.reshape(1, -1)))
    other_half = lax.ppermute(sent, "img", partners)
    other_back = pl.pallas_call(
        functools.partial(other_terms_kernel, rows),
        name="other_terms",
        out_shape=shape,
        in_specs=vmem(1),
        out_specs=vmem(1)[0],
        scratch_shapes=tables,
        compiler_params=limit,
        cost_estimate=pl.CostEstimate(flops=1, bytes_accessed=1, transcendentals=0),
    )(other_half)
    both = pl.pallas_call(
        back_kernel,
        name="back",
        out_shape=jax.ShapeDtypeStruct((chips, 2 * rows + PAD, COLS), BF),
        in_specs=vmem(5),
        out_specs=vmem(1)[0],
        compiler_params=limit,
    )(half, other_half, stats, back, other_back)
    same_core = [[2 * y + c for y in range(chips)] for c in range(2)]
    parts = lax.all_to_all(both, "img", 0, 0, tiled=True, axis_index_groups=same_core)
    reconstruction, evidence = pl.pallas_call(
        last_kernel,
        name="last",
        out_shape=(
            jax.ShapeDtypeStruct((rows, COLS), BF),
            jax.ShapeDtypeStruct((1, count), F32),
        ),
        in_specs=vmem(2),
        out_specs=tuple([pl.BlockSpec(memory_space=pltpu.HBM)] * 2),
        scratch_shapes=[
            pltpu.VMEM((rows, COLS), BF),
            pltpu.VMEM((1, count), F32),
            pltpu.SemaphoreType.DMA((2,)),
        ],
        compiler_params=limit,
    )(parts, chosen)
    return reconstruction, evidence.reshape(count)


def solution(mesh):
    placed = (P("img", None), P("proj", None), P(), P("img"), P("img"), P("img"), P())
    return jax.shard_map(
        shards, mesh=mesh, in_specs=placed, out_specs=(P("proj", "img"), P("img")), check_vma=False
    )
```

```python
import functools
import math

import jax
import jax.numpy as jnp
from jax import lax
from jax.experimental import pallas as pl
from jax.experimental.pallas import tpu as pltpu
from jax.sharding import PartitionSpec as P

F = 4096
BLOCK = 32
LANES = 128
COLS = 256
PAD = 8
NONE = -1e30
BF = jnp.bfloat16
F32 = jnp.float32


def small_sin_cos(x):
    y = x * x
    s = 1.0
    for k in (12, 10, 8, 6, 4, 2):
        s = 1.0 - y * s * (1.0 / (k * (k + 1)))
    c = 1.0
    for k in (14, 12, 10, 8, 6, 4, 2):
        c = 1.0 - y * c * (1.0 / (k * (k - 1)))
    return x * s, c


def down_rows(row):
    n = row.shape[1]
    return jnp.transpose(jnp.broadcast_to(row, (n, n)))


def set_turn(defocus, limits, turn, edge):
    images = turn.shape[1]
    lane = lax.broadcasted_iota(jnp.int32, (images, LANES), 1).astype(F32)
    angle = down_rows(defocus) * ((lane + 1.0) * (2.0 * math.pi / F))
    base_s, base_c = small_sin_cos(angle)
    first_s = base_s * math.cos(0.1) + base_c * math.sin(0.1)
    first_c = base_c * math.cos(0.1) - base_s * math.sin(0.1)
    step_s = jnp.broadcast_to(base_s[:, LANES - 1 :], (images, LANES))
    step_c = jnp.broadcast_to(base_c[:, LANES - 1 :], (images, LANES))
    turn[0] = first_s
    turn[1] = first_s * step_c - first_c * step_s
    turn[2] = step_c + step_c
    edge[...] = down_rows(limits.astype(F32)) - lane


def walk(g, pixels, turn, edge, use):
    for r in range(0, pixels.shape[0], 16):
        some = slice(r, r + 16)
        s, before = turn[0, some], turn[1, some]
        twice = turn[2, some]
        last = edge[some]
        for h in range(COLS // LANES):
            first = g * COLS + h * LANES
            at = slice(first, first + LANES)
            kept = jnp.where(last > float(first), s, 0.0)
            use(some, at, slice(h * LANES, (h + 1) * LANES), kept * pixels[some, at].astype(F32), kept * s)
            s, before = twice * s - before, s
        turn[0, some], turn[1, some] = s, before


def thirds(x):
    first = x.astype(BF)
    rest = x - first.astype(F32)
    second = rest.astype(BF)
    return first, second, (rest - second.astype(F32)).astype(BF)


def score_kernel(
    far_defocus, far_limits, far_pixels, far_proj, far_noise, far_counts, kept, sent, far_stats,
    defocus, limits, pixels, proj, noise, counts, terms, terms_sq, stats, turn, edge, arrived, left,
):
    rows, images = proj.shape[0], pixels.shape[0]
    copies = [
        pltpu.make_async_copy(far, near, arrived.at[k])
        for k, (far, near) in enumerate(
            (
                (far_defocus, defocus),
                (far_limits, limits),
                (far_pixels, pixels),
                (far_proj, proj),
                (far_noise, noise),
                (far_counts, counts),
            )
        )
    ]
    for copy in copies:
        copy.start()
    for copy in copies[:2]:
        copy.wait()
    set_turn(defocus[...], limits[...], turn, edge)
    for copy in copies[2:]:
        copy.wait()

    def use(some, at, inner, image, square):
        weight = noise[:, at]
        terms[some, at] = (weight * image).astype(BF)
        terms_sq[some, at] = ((-0.5 * weight) * square).astype(BF)

    sums = [jnp.zeros((rows, images), F32) for _ in range(4)]
    contract = (((1,), (1,)), ((), ()))
    for g in range(F // COLS):
        walk(g, pixels, turn, edge, use)
        at = slice(g * COLS, (g + 1) * COLS)
        some_proj = proj[:, at]
        wide = some_proj.astype(F32)
        sums[g % 2] += lax.dot_general(some_proj, terms[:, at], contract, preferred_element_type=F32)
        sums[2 + g % 2] += lax.dot_general((wide * wide).astype(BF), terms_sq[:, at], contract, preferred_element_type=F32)
    total = (sums[0] + sums[1]) + (sums[2] + sums[3])
    orient = lax.axis_index("proj") * rows + lax.broadcasted_iota(jnp.int32, (rows, images), 0)
    significant = orient < counts[...]
    found = jnp.where(significant, total, NONE)
    peak = jnp.max(found, axis=0, keepdims=True)
    mass = jnp.sum(jnp.where(significant, jnp.exp(found - peak), 0.0), axis=0, keepdims=True)
    both = jnp.concatenate([peak, mass], axis=0)
    stats[...] = jnp.broadcast_to(both[None], stats.shape)
    leaving = pltpu.make_async_copy(stats, far_stats, left)
    leaving.start()
    line = lax.broadcasted_iota(jnp.int32, (rows, images), 0)
    scalars = jnp.zeros((rows, images), F32)
    for k, part in enumerate((*thirds(defocus[...]), *thirds(limits[...].astype(F32)))):
        scalars = jnp.where(line == k, part.astype(F32), scalars)
    first, second, third = thirds(found)
    core = lax.rem(lax.axis_index("img"), 2)
    groups = F // COLS // 2
    tail = groups * images
    for out, side in ((kept, core), (sent, 1 - core)):
        for y in range(groups):
            at = pl.ds(pl.multiple_of((2 * y + side) * COLS, COLS), COLS)
            out[y * images : (y + 1) * images, :] = pixels[:, at]
        out[tail : tail + rows, :LANES] = first
        out[tail : tail + rows, LANES:] = second
        out[tail + rows :, :LANES] = third
        out[tail + rows :, LANES:] = scalars.astype(BF)
    leaving.wait()


def scores_of(half, rows):
    tail = half.shape[0] - 2 * rows
    first, second = half[tail : tail + rows, :LANES], half[tail : tail + rows, LANES:]
    return (first.astype(F32) + second.astype(F32)) + half[tail + rows :, :LANES].astype(F32)


def half_terms(half, rows, back, turn, edge):
    core = lax.rem(lax.axis_index("img"), 2)
    images = back.shape[2]
    start = half.shape[0] - rows
    scalars = half[start : start + 16, LANES:].astype(F32)
    focus, limits = ((scalars[k : k + 1] + scalars[k + 1 : k + 2]) + scalars[k + 2 : k + 3] for k in (0, 3))
    set_turn(focus, limits, turn, edge)
    for r in range(0, images, 16):
        some = slice(r, r + 16)
        s, before = turn[0, some], turn[1, some]
        twice = turn[2, some]
        one = twice * s - before
        two = twice * one - s
        s, before = jnp.where(core == 0, s, two), jnp.where(core == 0, before, one)
        last = edge[some] - (core * COLS).astype(F32)
        for y in range(back.shape[0]):
            for h in range(COLS // LANES):
                inner = slice(h * LANES, (h + 1) * LANES)
                kept = jnp.where(last > float(2 * y * COLS + h * LANES), s, 0.0)
                image = half[y * images + r : y * images + r + 16, inner].astype(F32)
                back[y, 0, some, inner] = (kept * image).astype(BF)
                back[y, 1, some, inner] = (kept * s).astype(BF)
                s, before = twice * s - before, s
            for h in range(COLS // LANES):
                s, before = twice * s - before, s


def other_terms_kernel(rows, half, back, turn, edge):
    half_terms(half, rows, back, turn, edge)


def own_terms_kernel(rows, half, far_plan, back, chosen, plan, turn, edge, arrived):
    copy = pltpu.make_async_copy(far_plan, plan, arrived)
    copy.start()
    half_terms(half, rows, back, turn, edge)
    copy.wait()
    per_line = LANES // BLOCK
    shape = chosen.shape[1:]
    blocks = plan.shape[1]
    line = lax.broadcasted_iota(jnp.int32, (shape[0], blocks), 0)
    number = lax.broadcasted_iota(jnp.int32, (shape[0], blocks), 1)
    group = lax.broadcasted_iota(jnp.int32, shape, 1) // BLOCK
    goal = jnp.broadcast_to(plan[...], (shape[0], blocks)).astype(F32)
    target = jnp.zeros(shape, F32)
    for k in range(per_line):
        mine = jnp.sum(jnp.where(number == line * per_line + k, goal, 0.0), axis=1, keepdims=True)
        target = jnp.where(group == k, mine, target)
    slot = (lax.axis_index("img") * per_line + group).astype(F32)
    for k in range(per_line):
        moved = target if k == 0 else pltpu.roll(target, k * BLOCK, 1)
        chosen[k] = jnp.where(moved == slot, 1.0, 0.0)


def evidence_of(stats):
    peaks, masses = stats[:, 0, :], stats[:, 1, :]
    peak = jnp.max(peaks, axis=0, keepdims=True)
    mass = jnp.sum(masses * jnp.exp(peaks - peak), axis=0, keepdims=True)
    return peak + jnp.log(mass)


def back_kernel(half, other_half, stats, back, other_back, out):
    rows = (out.shape[1] - PAD) // 4
    peers = stats.shape[0] // 2
    core = lax.rem(lax.axis_index("img"), 2)
    known = [evidence_of(stats[c * peers : (c + 1) * peers]) for c in range(2)]
    mine, other = jnp.where(core == 0, known[0], known[1]), jnp.where(core == 0, known[1], known[0])

    def posterior_of(scores, evidence):
        return jnp.where(scores > 0.5 * NONE, jnp.exp(scores - evidence), 0.0).astype(BF)

    posterior = posterior_of(scores_of(half, rows), mine)
    other_posterior = posterior_of(scores_of(other_half, rows), other)
    line = lax.broadcasted_iota(jnp.int32, (PAD, LANES), 0)
    note = jnp.zeros((PAD, LANES), F32)
    for c in range(2):
        for k, part in enumerate(thirds(known[c])):
            note = jnp.where(line == 2 * k + c, part.astype(F32), note)
    note = note.astype(BF)
    for y in range(out.shape[0]):
        for k in range(2):
            part = jnp.dot(posterior, back[y, k], preferred_element_type=F32)
            part += jnp.dot(other_posterior, other_back[y, k], preferred_element_type=F32)
            part = part.astype(BF)
            out[y, 2 * k * rows : (2 * k + 1) * rows, :] = part[:, :LANES]
            out[y, (2 * k + 1) * rows : (2 * k + 2) * rows, :] = part[:, LANES:]
        out[y, 4 * rows :, :] = note


def last_kernel(parts, chosen, far_reconstruction, far_evidence, reconstruction, evidence, sent):
    rows = reconstruction.shape[0]
    chips = parts.shape[0]
    for h in range(2):
        images, weights = (
            sum(parts[y, (2 * k + h) * rows : (2 * k + h + 1) * rows, :].astype(F32) for y in range(chips))
            for k in range(2)
        )
        reconstruction[:, h * LANES : (h + 1) * LANES] = (images / (weights + 1.0)).astype(BF)
    first = pltpu.make_async_copy(reconstruction, far_reconstruction, sent.at[0])
    first.start()
    lines = []
    for y in range(chips):
        note = parts[y, 4 * rows :, :].astype(F32)
        lines += [(note[c : c + 1] + note[c + 2 : c + 3]) + note[c + 4 : c + 5] for c in range(2)]
    known = jnp.concatenate(lines, axis=0)
    placed = jnp.zeros((1, LANES), F32)
    for k in range(LANES // BLOCK):
        moved = known if k == 0 else pltpu.roll(known, k * BLOCK, 1)
        placed += jnp.sum(jnp.where(chosen[k] > 0.0, moved, 0.0), axis=0, keepdims=True)
    evidence[...] = placed
    second = pltpu.make_async_copy(evidence, far_evidence, sent.at[1])
    second.start()
    first.wait()
    second.wait()


def kept_far(array):
    return pltpu.with_memory_space_constraint(array, pltpu.HBM)


def vmem(n):
    return [pl.BlockSpec(memory_space=pltpu.VMEM)] * n


def shards(images, projections, noise_weight, defocus, orient_count, term_limit, block_plan):
    rows, count = projections.shape[0], images.shape[0]
    devices, peers = lax.axis_size("img"), lax.axis_size("proj")
    chips = devices // 2
    limit = pltpu.CompilerParams(vmem_limit_bytes=16 * 2**20)
    focus, counts, limits = (a.reshape(1, count) for a in (defocus, orient_count, term_limit))
    tables = [pltpu.VMEM((3, count, LANES), F32), pltpu.VMEM((count, LANES), F32)]
    partners = [(i, i ^ 1) for i in range(devices)]
    operands = (focus, limits, images, projections, noise_weight.reshape(1, F), counts)
    shape = jax.ShapeDtypeStruct((chips * count + 2 * rows, COLS), BF)
    half, sent, stats = pl.pallas_call(
        score_kernel,
        name="score",
        out_shape=(
            shape,
            shape,
            jax.ShapeDtypeStruct((2 * peers, 2, count), F32),
        ),
        in_specs=[pl.BlockSpec(memory_space=pltpu.HBM)] * 6,
        out_specs=(*vmem(2), pl.BlockSpec(memory_space=pltpu.HBM)),
        scratch_shapes=[
            *(pltpu.VMEM(a.shape, a.dtype) for a in operands),
            pltpu.VMEM((count, F), BF),
            pltpu.VMEM((count, F), BF),
            pltpu.VMEM((2 * peers, 2, count), F32),
            *tables,
            pltpu.SemaphoreType.DMA((6,)),
            pltpu.SemaphoreType.DMA,
        ],
        compiler_params=limit,
    )(*map(kept_far, operands))
    chip = [[2 * y * peers + n for n in range(2 * peers)] for y in range(chips)]
    stats = lax.all_to_all(stats, ("img", "proj"), 0, 0, tiled=True, axis_index_groups=chip)
    shape = jax.ShapeDtypeStruct((chips, 2, count, COLS), BF)
    cost = pl.CostEstimate(flops=10**10, bytes_accessed=3 * count * F, transcendentals=0)
    back, chosen = pl.pallas_call(
        functools.partial(own_terms_kernel, rows),
        name="own_terms",
        out_shape=(shape, jax.ShapeDtypeStruct((LANES // BLOCK, devices, LANES), F32)),
        in_specs=[*vmem(1), pl.BlockSpec(memory_space=pltpu.HBM)],
        out_specs=tuple(vmem(2)),
        scratch_shapes=[pltpu.VMEM((1, block_plan.shape[0]), jnp.int32), *tables, pltpu.SemaphoreType.DMA],
        compiler_params=limit,
        cost_estimate=cost,
    )(half, kept_far(block_plan.reshape(1, -1)))
    other_half = lax.ppermute(sent, "img", partners)
    other_back = pl.pallas_call(
        functools.partial(other_terms_kernel, rows),
        name="other_terms",
        out_shape=shape,
        in_specs=vmem(1),
        out_specs=vmem(1)[0],
        scratch_shapes=tables,
        compiler_params=limit,
        cost_estimate=pl.CostEstimate(flops=1, bytes_accessed=1, transcendentals=0),
    )(other_half)
    both = pl.pallas_call(
        back_kernel,
        name="back",
        out_shape=jax.ShapeDtypeStruct((chips, 4 * rows + PAD, LANES), BF),
        in_specs=vmem(5),
        out_specs=vmem(1)[0],
        compiler_params=limit,
    )(half, other_half, stats, back, other_back)
    same_core = [[2 * y + c for y in range(chips)] for c in range(2)]
    parts = lax.all_to_all(both, "img", 0, 0, tiled=True, axis_index_groups=same_core)
    reconstruction, evidence = pl.pallas_call(
        last_kernel,
        name="last",
        out_shape=(
            jax.ShapeDtypeStruct((rows, COLS), BF),
            jax.ShapeDtypeStruct((1, count), F32),
        ),
        in_specs=vmem(2),
        out_specs=tuple([pl.BlockSpec(memory_space=pltpu.HBM)] * 2),
        scratch_shapes=[
            pltpu.VMEM((rows, COLS), BF),
            pltpu.VMEM((1, count), F32),
            pltpu.SemaphoreType.DMA((2,)),
        ],
        compiler_params=limit,
    )(parts, chosen)
    return reconstruction, evidence.reshape(count)


def solution(mesh):
    placed = (P("img", None), P("proj", None), P(), P("img"), P("img"), P("img"), P())
    return jax.shard_map(
        shards, mesh=mesh, in_specs=placed, out_specs=(P("proj", "img"), P("img")), check_vma=False
    )
```

```python
import functools
import math

import jax
import jax.numpy as jnp
from jax import lax
from jax.experimental import pallas as pl
from jax.experimental.pallas import tpu as pltpu
from jax.sharding import PartitionSpec as P

F = 4096
BLOCK = 32
LANES = 128
COLS = 256
PAD = 8
NONE = -1e30
BF = jnp.bfloat16
F32 = jnp.float32


def small_sin_cos(x):
    y = x * x
    s = 1.0
    for k in (12, 10, 8, 6, 4, 2):
        s = 1.0 - y * s * (1.0 / (k * (k + 1)))
    c = 1.0
    for k in (14, 12, 10, 8, 6, 4, 2):
        c = 1.0 - y * c * (1.0 / (k * (k - 1)))
    return x * s, c


def down_rows(row):
    n = row.shape[1]
    return jnp.transpose(jnp.broadcast_to(row, (n, n)))


def set_turn(defocus, limits, turn, edge):
    images = turn.shape[1]
    lane = lax.broadcasted_iota(jnp.int32, (images, LANES), 1).astype(F32)
    angle = down_rows(defocus) * ((lane + 1.0) * (2.0 * math.pi / F))
    base_s, base_c = small_sin_cos(angle)
    first_s = base_s * math.cos(0.1) + base_c * math.sin(0.1)
    first_c = base_c * math.cos(0.1) - base_s * math.sin(0.1)
    step_s = jnp.broadcast_to(base_s[:, LANES - 1 :], (images, LANES))
    step_c = jnp.broadcast_to(base_c[:, LANES - 1 :], (images, LANES))
    turn[0] = first_s
    turn[1] = first_s * step_c - first_c * step_s
    turn[2] = step_c + step_c
    edge[...] = down_rows(limits.astype(F32)) - lane


def walk(g, pixels, turn, edge, use):
    for r in range(0, pixels.shape[0], 16):
        some = slice(r, r + 16)
        s, before = turn[0, some], turn[1, some]
        twice = turn[2, some]
        last = edge[some]
        for h in range(COLS // LANES):
            first = g * COLS + h * LANES
            at = slice(first, first + LANES)
            kept = jnp.where(last > float(first), s, 0.0)
            use(some, at, slice(h * LANES, (h + 1) * LANES), kept * pixels[some, at].astype(F32), kept * s)
            s, before = twice * s - before, s
        turn[0, some], turn[1, some] = s, before


def thirds(x):
    first = x.astype(BF)
    rest = x - first.astype(F32)
    second = rest.astype(BF)
    return first, second, (rest - second.astype(F32)).astype(BF)


def score_kernel(
    far_defocus, far_limits, far_pixels, far_proj, far_noise, far_counts, kept, sent, far_stats,
    defocus, limits, pixels, proj, noise, counts, terms, terms_sq, stats, turn, edge, arrived, left,
):
    rows, images = proj.shape[0], pixels.shape[0]
    copies = [
        pltpu.make_async_copy(far, near, arrived.at[k])
        for k, (far, near) in enumerate(
            (
                (far_defocus, defocus),
                (far_limits, limits),
                (far_pixels, pixels),
                (far_proj, proj),
                (far_noise, noise),
                (far_counts, counts),
            )
        )
    ]
    for copy in copies:
        copy.start()
    for copy in copies[:2]:
        copy.wait()
    set_turn(defocus[...], limits[...], turn, edge)
    for copy in copies[2:]:
        copy.wait()

    def use(some, at, inner, image, square):
        weight = noise[:, at]
        terms[some, at] = (weight * image).astype(BF)
        terms_sq[some, at] = ((-0.5 * weight) * square).astype(BF)

    sums = [jnp.zeros((rows, images), F32) for _ in range(4)]
    contract = (((1,), (1,)), ((), ()))
    for g in range(F // COLS):
        walk(g, pixels, turn, edge, use)
        at = slice(g * COLS, (g + 1) * COLS)
        some_proj = proj[:, at]
        wide = some_proj.astype(F32)
        sums[g % 2] += lax.dot_general(some_proj, terms[:, at], contract, preferred_element_type=F32)
        sums[2 + g % 2] += lax.dot_general((wide * wide).astype(BF), terms_sq[:, at], contract, preferred_element_type=F32)
    total = (sums[0] + sums[1]) + (sums[2] + sums[3])
    orient = lax.axis_index("proj") * rows + lax.broadcasted_iota(jnp.int32, (rows, images), 0)
    significant = orient < counts[...]
    found = jnp.where(significant, total, NONE)
    peak = jnp.max(found, axis=0, keepdims=True)
    mass = jnp.sum(jnp.where(significant, jnp.exp(found - peak), 0.0), axis=0, keepdims=True)
    local = jnp.where(mass > 0.0, peak + jnp.log(mass), NONE)
    stats[...] = jnp.broadcast_to(local[None], stats.shape)
    leaving = pltpu.make_async_copy(stats, far_stats, left)
    leaving.start()
    line = lax.broadcasted_iota(jnp.int32, (rows, images), 0)
    scalars = jnp.zeros((rows, images), F32)
    for k, part in enumerate((*thirds(defocus[...]), *thirds(limits[...].astype(F32)))):
        scalars = jnp.where(line == k, part.astype(F32), scalars)
    first, second, third = thirds(found)
    core = lax.rem(lax.axis_index("img"), 2)
    groups = F // COLS // 2
    tail = groups * images
    for out, side in ((kept, core), (sent, 1 - core)):
        for y in range(groups):
            at = pl.ds(pl.multiple_of((2 * y + side) * COLS, COLS), COLS)
            out[y * images : (y + 1) * images, :] = pixels[:, at]
        out[tail : tail + rows, :LANES] = first
        out[tail : tail + rows, LANES:] = second
        out[tail + rows :, :LANES] = third
        out[tail + rows :, LANES:] = scalars.astype(BF)
    leaving.wait()


def scores_of(half, rows):
    tail = half.shape[0] - 2 * rows
    first, second = half[tail : tail + rows, :LANES], half[tail : tail + rows, LANES:]
    return (first.astype(F32) + second.astype(F32)) + half[tail + rows :, :LANES].astype(F32)


def half_terms(half, rows, back, turn, edge):
    core = lax.rem(lax.axis_index("img"), 2)
    images = back.shape[2]
    start = half.shape[0] - rows
    scalars = half[start : start + 16, LANES:].astype(F32)
    focus, limits = ((scalars[k : k + 1] + scalars[k + 1 : k + 2]) + scalars[k + 2 : k + 3] for k in (0, 3))
    set_turn(focus, limits, turn, edge)
    for r in range(0, images, 16):
        some = slice(r, r + 16)
        s, before = turn[0, some], turn[1, some]
        twice = turn[2, some]
        one = twice * s - before
        two = twice * one - s
        s, before = jnp.where(core == 0, s, two), jnp.where(core == 0, before, one)
        last = edge[some] - (core * COLS).astype(F32)
        for y in range(back.shape[0]):
            for h in range(COLS // LANES):
                inner = slice(h * LANES, (h + 1) * LANES)
                kept = jnp.where(last > float(2 * y * COLS + h * LANES), s, 0.0)
                image = half[y * images + r : y * images + r + 16, inner].astype(F32)
                back[y, 0, some, inner] = (kept * image).astype(BF)
                back[y, 1, some, inner] = (kept * s).astype(BF)
                s, before = twice * s - before, s
            for h in range(COLS // LANES):
                s, before = twice * s - before, s


def other_terms_kernel(rows, half, back, turn, edge):
    half_terms(half, rows, back, turn, edge)


def own_terms_kernel(rows, half, far_plan, back, chosen, plan, turn, edge, arrived):
    copy = pltpu.make_async_copy(far_plan, plan, arrived)
    copy.start()
    half_terms(half, rows, back, turn, edge)
    copy.wait()
    per_line = LANES // BLOCK
    shape = chosen.shape[1:]
    blocks = plan.shape[1]
    line = lax.broadcasted_iota(jnp.int32, (shape[0], blocks), 0)
    number = lax.broadcasted_iota(jnp.int32, (shape[0], blocks), 1)
    group = lax.broadcasted_iota(jnp.int32, shape, 1) // BLOCK
    goal = jnp.broadcast_to(plan[...], (shape[0], blocks)).astype(F32)
    target = jnp.zeros(shape, F32)
    for k in range(per_line):
        mine = jnp.sum(jnp.where(number == line * per_line + k, goal, 0.0), axis=1, keepdims=True)
        target = jnp.where(group == k, mine, target)
    slot = (lax.axis_index("img") * per_line + group).astype(F32)
    for k in range(per_line):
        moved = target if k == 0 else pltpu.roll(target, k * BLOCK, 1)
        chosen[k] = jnp.where(moved == slot, 1.0, 0.0)


def evidence_of(stats):
    local = stats[:, 0, :]
    peak = jnp.max(local, axis=0, keepdims=True)
    return peak + jnp.log(jnp.sum(jnp.exp(local - peak), axis=0, keepdims=True))


def back_kernel(half, other_half, stats, back, other_back, out):
    rows = (out.shape[1] - PAD) // 4
    peers = stats.shape[0] // 2
    core = lax.rem(lax.axis_index("img"), 2)
    known = [evidence_of(stats[c * peers : (c + 1) * peers]) for c in range(2)]
    mine, other = jnp.where(core == 0, known[0], known[1]), jnp.where(core == 0, known[1], known[0])

    def posterior_of(scores, evidence):
        return jnp.where(scores > 0.5 * NONE, jnp.exp(scores - evidence), 0.0).astype(BF)

    posterior = posterior_of(scores_of(half, rows), mine)
    other_posterior = posterior_of(scores_of(other_half, rows), other)
    line = lax.broadcasted_iota(jnp.int32, (PAD, LANES), 0)
    note = jnp.zeros((PAD, LANES), F32)
    for c in range(2):
        for k, part in enumerate(thirds(known[c])):
            note = jnp.where(line == 2 * k + c, part.astype(F32), note)
    note = note.astype(BF)
    for y in range(out.shape[0]):
        for k in range(2):
            part = jnp.dot(posterior, back[y, k], preferred_element_type=F32)
            part += jnp.dot(other_posterior, other_back[y, k], preferred_element_type=F32)
            part = part.astype(BF)
            out[y, 2 * k * rows : (2 * k + 1) * rows, :] = part[:, :LANES]
            out[y, (2 * k + 1) * rows : (2 * k + 2) * rows, :] = part[:, LANES:]
        out[y, 4 * rows :, :] = note


def last_kernel(parts, chosen, far_reconstruction, far_evidence, reconstruction, evidence, sent):
    rows = reconstruction.shape[0]
    chips = parts.shape[0]
    for h in range(2):
        images, weights = (
            sum(parts[y, (2 * k + h) * rows : (2 * k + h + 1) * rows, :].astype(F32) for y in range(chips))
            for k in range(2)
        )
        reconstruction[:, h * LANES : (h + 1) * LANES] = (images / (weights + 1.0)).astype(BF)
    first = pltpu.make_async_copy(reconstruction, far_reconstruction, sent.at[0])
    first.start()
    lines = []
    for y in range(chips):
        note = parts[y, 4 * rows :, :].astype(F32)
        lines += [(note[c : c + 1] + note[c + 2 : c + 3]) + note[c + 4 : c + 5] for c in range(2)]
    known = jnp.concatenate(lines, axis=0)
    placed = jnp.zeros((1, LANES), F32)
    for k in range(LANES // BLOCK):
        moved = known if k == 0 else pltpu.roll(known, k * BLOCK, 1)
        placed += jnp.sum(jnp.where(chosen[k] > 0.0, moved, 0.0), axis=0, keepdims=True)
    evidence[...] = placed
    second = pltpu.make_async_copy(evidence, far_evidence, sent.at[1])
    second.start()
    first.wait()
    second.wait()


def kept_far(array):
    return pltpu.with_memory_space_constraint(array, pltpu.HBM)


def vmem(n):
    return [pl.BlockSpec(memory_space=pltpu.VMEM)] * n


def shards(images, projections, noise_weight, defocus, orient_count, term_limit, block_plan):
    rows, count = projections.shape[0], images.shape[0]
    devices, peers = lax.axis_size("img"), lax.axis_size("proj")
    chips = devices // 2
    limit = pltpu.CompilerParams(vmem_limit_bytes=16 * 2**20)
    focus, counts, limits = (a.reshape(1, count) for a in (defocus, orient_count, term_limit))
    tables = [pltpu.VMEM((3, count, LANES), F32), pltpu.VMEM((count, LANES), F32)]
    partners = [(i, i ^ 1) for i in range(devices)]
    operands = (focus, limits, images, projections, noise_weight.reshape(1, F), counts)
    shape = jax.ShapeDtypeStruct((chips * count + 2 * rows, COLS), BF)
    half, sent, stats = pl.pallas_call(
        score_kernel,
        name="score",
        out_shape=(
            shape,
            shape,
            jax.ShapeDtypeStruct((2 * peers, 1, count), F32),
        ),
        in_specs=[pl.BlockSpec(memory_space=pltpu.HBM)] * 6,
        out_specs=(*vmem(2), pl.BlockSpec(memory_space=pltpu.HBM)),
        scratch_shapes=[
            *(pltpu.VMEM(a.shape, a.dtype) for a in operands),
            pltpu.VMEM((count, F), BF),
            pltpu.VMEM((count, F), BF),
            pltpu.VMEM((2 * peers, 1, count), F32),
            *tables,
            pltpu.SemaphoreType.DMA((6,)),
            pltpu.SemaphoreType.DMA,
        ],
        compiler_params=limit,
    )(*map(kept_far, operands))
    chip = [[2 * y * peers + n for n in range(2 * peers)] for y in range(chips)]
    stats = lax.all_to_all(stats, ("img", "proj"), 0, 0, tiled=True, axis_index_groups=chip)
    shape = jax.ShapeDtypeStruct((chips, 2, count, COLS), BF)
    cost = pl.CostEstimate(flops=10**10, bytes_accessed=3 * count * F, transcendentals=0)
    back, chosen = pl.pallas_call(
        functools.partial(own_terms_kernel, rows),
        name="own_terms",
        out_shape=(shape, jax.ShapeDtypeStruct((LANES // BLOCK, devices, LANES), F32)),
        in_specs=[*vmem(1), pl.BlockSpec(memory_space=pltpu.HBM)],
        out_specs=tuple(vmem(2)),
        scratch_shapes=[pltpu.VMEM((1, block_plan.shape[0]), jnp.int32), *tables, pltpu.SemaphoreType.DMA],
        compiler_params=limit,
        cost_estimate=cost,
    )(half, kept_far(block_plan.reshape(1, -1)))
    other_half = lax.ppermute(sent, "img", partners)
    other_back = pl.pallas_call(
        functools.partial(other_terms_kernel, rows),
        name="other_terms",
        out_shape=shape,
        in_specs=vmem(1),
        out_specs=vmem(1)[0],
        scratch_shapes=tables,
        compiler_params=limit,
        cost_estimate=pl.CostEstimate(flops=1, bytes_accessed=1, transcendentals=0),
    )(other_half)
    both = pl.pallas_call(
        back_kernel,
        name="back",
        out_shape=jax.ShapeDtypeStruct((chips, 4 * rows + PAD, LANES), BF),
        in_specs=vmem(5),
        out_specs=vmem(1)[0],
        compiler_params=limit,
    )(half, other_half, stats, back, other_back)
    same_core = [[2 * y + c for y in range(chips)] for c in range(2)]
    parts = lax.all_to_all(both, "img", 0, 0, tiled=True, axis_index_groups=same_core)
    reconstruction, evidence = pl.pallas_call(
        last_kernel,
        name="last",
        out_shape=(
            jax.ShapeDtypeStruct((rows, COLS), BF),
            jax.ShapeDtypeStruct((1, count), F32),
        ),
        in_specs=vmem(2),
        out_specs=tuple([pl.BlockSpec(memory_space=pltpu.HBM)] * 2),
        scratch_shapes=[
            pltpu.VMEM((rows, COLS), BF),
            pltpu.VMEM((1, count), F32),
            pltpu.SemaphoreType.DMA((2,)),
        ],
        compiler_params=limit,
    )(parts, chosen)
    return reconstruction, evidence.reshape(count)


def solution(mesh):
    placed = (P("img", None), P("proj", None), P(), P("img"), P("img"), P("img"), P())
    return jax.shard_map(
        shards, mesh=mesh, in_specs=placed, out_specs=(P("proj", "img"), P("img")), check_vma=False
    )
```

```python
import functools
import math

import jax
import jax.numpy as jnp
from jax import lax
from jax.experimental import pallas as pl
from jax.experimental.pallas import tpu as pltpu
from jax.sharding import PartitionSpec as P

F = 4096
BLOCK = 32
LANES = 128
COLS = 256
PAD = 8
NONE = -1e30
BF = jnp.bfloat16
F32 = jnp.float32


def small_sin_cos(x):
    y = x * x
    s = 1.0
    for k in (12, 10, 8, 6, 4, 2):
        s = 1.0 - y * s * (1.0 / (k * (k + 1)))
    c = 1.0
    for k in (14, 12, 10, 8, 6, 4, 2):
        c = 1.0 - y * c * (1.0 / (k * (k - 1)))
    return x * s, c


def down_rows(row):
    n = row.shape[1]
    return jnp.transpose(jnp.broadcast_to(row, (n, n)))


def set_turn(defocus, limits, turn, edge):
    images = turn.shape[1]
    lane = lax.broadcasted_iota(jnp.int32, (images, LANES), 1).astype(F32)
    angle = down_rows(defocus) * ((lane + 1.0) * (2.0 * math.pi / F))
    base_s, base_c = small_sin_cos(angle)
    first_s = base_s * math.cos(0.1) + base_c * math.sin(0.1)
    first_c = base_c * math.cos(0.1) - base_s * math.sin(0.1)
    step_s = jnp.broadcast_to(base_s[:, LANES - 1 :], (images, LANES))
    step_c = jnp.broadcast_to(base_c[:, LANES - 1 :], (images, LANES))
    turn[0] = first_s
    turn[1] = first_s * step_c - first_c * step_s
    turn[2] = step_c + step_c
    edge[...] = down_rows(limits.astype(F32)) - lane


def walk(g, pixels, turn, edge, use):
    for r in range(0, pixels.shape[0], 16):
        some = slice(r, r + 16)
        s, before = turn[0, some], turn[1, some]
        twice = turn[2, some]
        last = edge[some]
        for h in range(COLS // LANES):
            first = g * COLS + h * LANES
            at = slice(first, first + LANES)
            kept = jnp.where(last > float(first), s, 0.0)
            use(some, at, slice(h * LANES, (h + 1) * LANES), kept * pixels[some, at].astype(F32), kept * s)
            s, before = twice * s - before, s
        turn[0, some], turn[1, some] = s, before


def thirds(x):
    first = x.astype(BF)
    rest = x - first.astype(F32)
    second = rest.astype(BF)
    return first, second, (rest - second.astype(F32)).astype(BF)


def score_kernel(
    far_defocus, far_limits, far_pixels, far_proj, far_noise, far_counts, kept, sent, far_stats,
    defocus, limits, pixels, proj, noise, counts, terms, terms_sq, stats, turn, edge, arrived, left,
):
    rows, images = proj.shape[0], pixels.shape[0]
    copies = [
        pltpu.make_async_copy(far, near, arrived.at[k])
        for k, (far, near) in enumerate(
            (
                (far_defocus, defocus),
                (far_limits, limits),
                (far_pixels, pixels),
                (far_proj, proj),
                (far_noise, noise),
                (far_counts, counts),
            )
        )
    ]
    for copy in copies:
        copy.start()
    for copy in copies[:2]:
        copy.wait()
    set_turn(defocus[...], limits[...], turn, edge)
    for copy in copies[2:]:
        copy.wait()

    def use(some, at, inner, image, square):
        weight = noise[:, at]
        terms[some, at] = (weight * image).astype(BF)
        terms_sq[some, at] = ((-0.5 * weight) * square).astype(BF)

    sums = [jnp.zeros((rows, images), F32) for _ in range(4)]
    contract = (((1,), (1,)), ((), ()))
    for g in range(F // COLS):
        walk(g, pixels, turn, edge, use)
        at = slice(g * COLS, (g + 1) * COLS)
        some_proj = proj[:, at]
        wide = some_proj.astype(F32)
        sums[g % 2] += lax.dot_general(some_proj, terms[:, at], contract, preferred_element_type=F32)
        sums[2 + g % 2] += lax.dot_general((wide * wide).astype(BF), terms_sq[:, at], contract, preferred_element_type=F32)
    total = (sums[0] + sums[1]) + (sums[2] + sums[3])
    orient = lax.axis_index("proj") * rows + lax.broadcasted_iota(jnp.int32, (rows, images), 0)
    significant = orient < counts[...]
    found = jnp.where(significant, total, NONE)
    peak = jnp.max(found, axis=0, keepdims=True)
    mass = jnp.sum(jnp.where(significant, jnp.exp(found - peak), 0.0), axis=0, keepdims=True)
    local = jnp.where(mass > 0.0, peak + jnp.log(mass), NONE)
    stats[...] = jnp.broadcast_to(local[None], stats.shape)
    leaving = pltpu.make_async_copy(stats, far_stats, left)
    leaving.start()
    line = lax.broadcasted_iota(jnp.int32, (rows, images), 0)
    scalars = jnp.zeros((rows, images), F32)
    for k, part in enumerate((*thirds(defocus[...]), *thirds(limits[...].astype(F32)))):
        scalars = jnp.where(line == k, part.astype(F32), scalars)
    first, second, third = thirds(found)
    core = lax.rem(lax.axis_index("img"), 2)
    groups = F // COLS // 2
    tail = groups * images
    for out, side in ((kept, core), (sent, 1 - core)):
        for y in range(groups):
            at = pl.ds(pl.multiple_of((2 * y + side) * COLS, COLS), COLS)
            out[y * images : (y + 1) * images, :] = pixels[:, at]
        out[tail : tail + rows, :LANES] = first
        out[tail : tail + rows, LANES:] = second
        out[tail + rows :, :LANES] = third
        out[tail + rows :, LANES:] = scalars.astype(BF)
    leaving.wait()


def scores_of(half, rows):
    tail = half.shape[0] - 2 * rows
    first, second = half[tail : tail + rows, :LANES], half[tail : tail + rows, LANES:]
    return (first.astype(F32) + second.astype(F32)) + half[tail + rows :, :LANES].astype(F32)


def half_terms(half, rows, back, turn, edge):
    core = lax.rem(lax.axis_index("img"), 2)
    images = back.shape[2]
    start = half.shape[0] - rows
    scalars = half[start : start + 16, LANES:].astype(F32)
    focus, limits = ((scalars[k : k + 1] + scalars[k + 1 : k + 2]) + scalars[k + 2 : k + 3] for k in (0, 3))
    set_turn(focus, limits, turn, edge)
    for r in range(0, images, 16):
        some = slice(r, r + 16)
        s, before = turn[0, some], turn[1, some]
        twice = turn[2, some]
        one = twice * s - before
        two = twice * one - s
        s, before = jnp.where(core == 0, s, two), jnp.where(core == 0, before, one)
        last = edge[some] - (core * COLS).astype(F32)
        for y in range(back.shape[0]):
            for h in range(COLS // LANES):
                inner = slice(h * LANES, (h + 1) * LANES)
                kept = jnp.where(last > float(2 * y * COLS + h * LANES), s, 0.0)
                image = half[y * images + r : y * images + r + 16, inner].astype(F32)
                back[y, 0, some, inner] = (kept * image).astype(BF)
                back[y, 1, some, inner] = (kept * s).astype(BF)
                s, before = twice * s - before, s
            for h in range(COLS // LANES):
                s, before = twice * s - before, s


def other_terms_kernel(rows, half, back, turn, edge):
    half_terms(half, rows, back, turn, edge)


def own_terms_kernel(rows, half, far_plan, back, chosen, plan, turn, edge, arrived):
    copy = pltpu.make_async_copy(far_plan, plan, arrived)
    copy.start()
    half_terms(half, rows, back, turn, edge)
    copy.wait()
    per_line = LANES // BLOCK
    shape = chosen.shape[1:]
    blocks = plan.shape[1]
    line = lax.broadcasted_iota(jnp.int32, (shape[0], blocks), 0)
    number = lax.broadcasted_iota(jnp.int32, (shape[0], blocks), 1)
    group = lax.broadcasted_iota(jnp.int32, shape, 1) // BLOCK
    goal = jnp.broadcast_to(plan[...], (shape[0], blocks)).astype(F32)
    target = jnp.zeros(shape, F32)
    for k in range(per_line):
        mine = jnp.sum(jnp.where(number == line * per_line + k, goal, 0.0), axis=1, keepdims=True)
        target = jnp.where(group == k, mine, target)
    slot = (lax.axis_index("img") * per_line + group).astype(F32)
    for k in range(per_line):
        moved = target if k == 0 else pltpu.roll(target, k * BLOCK, 1)
        chosen[k] = jnp.where(moved == slot, 1.0, 0.0)


def evidence_of(stats):
    local = stats[:, 0, :]
    peak = jnp.max(local, axis=0, keepdims=True)
    return peak + jnp.log(jnp.sum(jnp.exp(local - peak), axis=0, keepdims=True))


def back_kernel(half, other_half, stats, back, other_back, out):
    rows = (out.shape[1] - PAD) // 4
    peers = stats.shape[0] // 2
    core = lax.rem(lax.axis_index("img"), 2)
    known = [evidence_of(stats[c * peers : (c + 1) * peers]) for c in range(2)]
    mine, other = jnp.where(core == 0, known[0], known[1]), jnp.where(core == 0, known[1], known[0])

    def posterior_of(scores, evidence):
        return jnp.where(scores > 0.5 * NONE, jnp.exp(scores - evidence), 0.0).astype(BF)

    posterior = jnp.concatenate(
        [posterior_of(scores_of(half, rows), mine), posterior_of(scores_of(other_half, rows), other)], axis=1
    )
    line = lax.broadcasted_iota(jnp.int32, (PAD, LANES), 0)
    note = jnp.zeros((PAD, LANES), F32)
    for c in range(2):
        for k, part in enumerate(thirds(known[c])):
            note = jnp.where(line == 2 * k + c, part.astype(F32), note)
    note = note.astype(BF)
    for y in range(out.shape[0]):
        for k in range(2):
            terms = jnp.concatenate([back[y, k], other_back[y, k]], axis=0)
            part = jnp.dot(posterior, terms, preferred_element_type=F32).astype(BF)
            out[y, 2 * k * rows : (2 * k + 1) * rows, :] = part[:, :LANES]
            out[y, (2 * k + 1) * rows : (2 * k + 2) * rows, :] = part[:, LANES:]
        out[y, 4 * rows :, :] = note


def last_kernel(parts, chosen, far_reconstruction, far_evidence, reconstruction, evidence, sent):
    rows = reconstruction.shape[0]
    chips = parts.shape[0]
    for h in range(2):
        images, weights = (
            sum(parts[y, (2 * k + h) * rows : (2 * k + h + 1) * rows, :].astype(F32) for y in range(chips))
            for k in range(2)
        )
        reconstruction[:, h * LANES : (h + 1) * LANES] = (images / (weights + 1.0)).astype(BF)
    first = pltpu.make_async_copy(reconstruction, far_reconstruction, sent.at[0])
    first.start()
    lines = []
    for y in range(chips):
        note = parts[y, 4 * rows :, :].astype(F32)
        lines += [(note[c : c + 1] + note[c + 2 : c + 3]) + note[c + 4 : c + 5] for c in range(2)]
    known = jnp.concatenate(lines, axis=0)
    placed = jnp.zeros((1, LANES), F32)
    for k in range(LANES // BLOCK):
        moved = known if k == 0 else pltpu.roll(known, k * BLOCK, 1)
        placed += jnp.sum(jnp.where(chosen[k] > 0.0, moved, 0.0), axis=0, keepdims=True)
    evidence[...] = placed
    second = pltpu.make_async_copy(evidence, far_evidence, sent.at[1])
    second.start()
    first.wait()
    second.wait()


def kept_far(array):
    return pltpu.with_memory_space_constraint(array, pltpu.HBM)


def vmem(n):
    return [pl.BlockSpec(memory_space=pltpu.VMEM)] * n


def shards(images, projections, noise_weight, defocus, orient_count, term_limit, block_plan):
    rows, count = projections.shape[0], images.shape[0]
    devices, peers = lax.axis_size("img"), lax.axis_size("proj")
    chips = devices // 2
    limit = pltpu.CompilerParams(vmem_limit_bytes=16 * 2**20)
    focus, counts, limits = (a.reshape(1, count) for a in (defocus, orient_count, term_limit))
    tables = [pltpu.VMEM((3, count, LANES), F32), pltpu.VMEM((count, LANES), F32)]
    partners = [(i, i ^ 1) for i in range(devices)]
    operands = (focus, limits, images, projections, noise_weight.reshape(1, F), counts)
    shape = jax.ShapeDtypeStruct((chips * count + 2 * rows, COLS), BF)
    half, sent, stats = pl.pallas_call(
        score_kernel,
        name="score",
        out_shape=(
            shape,
            shape,
            jax.ShapeDtypeStruct((2 * peers, 1, count), F32),
        ),
        in_specs=[pl.BlockSpec(memory_space=pltpu.HBM)] * 6,
        out_specs=(*vmem(2), pl.BlockSpec(memory_space=pltpu.HBM)),
        scratch_shapes=[
            *(pltpu.VMEM(a.shape, a.dtype) for a in operands),
            pltpu.VMEM((count, F), BF),
            pltpu.VMEM((count, F), BF),
            pltpu.VMEM((2 * peers, 1, count), F32),
            *tables,
            pltpu.SemaphoreType.DMA((6,)),
            pltpu.SemaphoreType.DMA,
        ],
        compiler_params=limit,
    )(*map(kept_far, operands))
    chip = [[2 * y * peers + n for n in range(2 * peers)] for y in range(chips)]
    stats = lax.all_to_all(stats, ("img", "proj"), 0, 0, tiled=True, axis_index_groups=chip)
    shape = jax.ShapeDtypeStruct((chips, 2, count, COLS), BF)
    cost = pl.CostEstimate(flops=10**10, bytes_accessed=3 * count * F, transcendentals=0)
    back, chosen = pl.pallas_call(
        functools.partial(own_terms_kernel, rows),
        name="own_terms",
        out_shape=(shape, jax.ShapeDtypeStruct((LANES // BLOCK, devices, LANES), F32)),
        in_specs=[*vmem(1), pl.BlockSpec(memory_space=pltpu.HBM)],
        out_specs=tuple(vmem(2)),
        scratch_shapes=[pltpu.VMEM((1, block_plan.shape[0]), jnp.int32), *tables, pltpu.SemaphoreType.DMA],
        compiler_params=limit,
        cost_estimate=cost,
    )(half, kept_far(block_plan.reshape(1, -1)))
    other_half = lax.ppermute(sent, "img", partners)
    other_back = pl.pallas_call(
        functools.partial(other_terms_kernel, rows),
        name="other_terms",
        out_shape=shape,
        in_specs=vmem(1),
        out_specs=vmem(1)[0],
        scratch_shapes=tables,
        compiler_params=limit,
        cost_estimate=pl.CostEstimate(flops=1, bytes_accessed=1, transcendentals=0),
    )(other_half)
    both = pl.pallas_call(
        back_kernel,
        name="back",
        out_shape=jax.ShapeDtypeStruct((chips, 4 * rows + PAD, LANES), BF),
        in_specs=vmem(5),
        out_specs=vmem(1)[0],
        compiler_params=limit,
    )(half, other_half, stats, back, other_back)
    same_core = [[2 * y + c for y in range(chips)] for c in range(2)]
    parts = lax.all_to_all(both, "img", 0, 0, tiled=True, axis_index_groups=same_core)
    reconstruction, evidence = pl.pallas_call(
        last_kernel,
        name="last",
        out_shape=(
            jax.ShapeDtypeStruct((rows, COLS), BF),
            jax.ShapeDtypeStruct((1, count), F32),
        ),
        in_specs=vmem(2),
        out_specs=tuple([pl.BlockSpec(memory_space=pltpu.HBM)] * 2),
        scratch_shapes=[
            pltpu.VMEM((rows, COLS), BF),
            pltpu.VMEM((1, count), F32),
            pltpu.SemaphoreType.DMA((2,)),
        ],
        compiler_params=limit,
    )(parts, chosen)
    return reconstruction, evidence.reshape(count)


def solution(mesh):
    placed = (P("img", None), P("proj", None), P(), P("img"), P("img"), P("img"), P())
    return jax.shard_map(
        shards, mesh=mesh, in_specs=placed, out_specs=(P("proj", "img"), P("img")), check_vma=False
    )
```
